256 devices in a mesh: sample: 16 (over z_hi, y, core), space: 16 (over x, z_lo).
Axes of the slice: x: 4, y: 4, z: 8 (z_hi: 2, z_lo: 4; z = z_hi * 4 + z_lo), core: 2. Of those that a mesh axis runs over, the one named last changes fastest.
Arguments:
- volume: bfloat16 [16, 4, 16, 8, 128], P('sample', None, 'space'), may hold values from -6 to 6
- cotangent: bfloat16 [16, 128, 16, 8, 128], P('sample', None, 'space'), may hold values from -6 to 6
- weight_one: bfloat16 [3, 3, 3, 4, 32], replicated, may hold values from -0.625 to 0.625
- bias_one: float32 [32], replicated, may hold values from -0.5 to 0.5
- weight_two: bfloat16 [3, 3, 3, 32, 64], replicated, may hold values from -0.21875 to 0.21875
- bias_two: float32 [64], replicated, may hold values from -0.5 to 0.5
- weight_three: bfloat16 [3, 3, 3, 64, 128], replicated, may hold values from -0.15625 to 0.15625
- bias_three: float32 [128], replicated, may hold values from -0.5 to 0.5
Outputs:
- grad_weight_one: float32 [3, 3, 3, 4, 32], replicated
- grad_bias_one: float32 [32], replicated
- grad_weight_two: float32 [3, 3, 3, 32, 64], replicated
- grad_bias_two: float32 [64], replicated
- grad_weight_three: float32 [3, 3, 3, 64, 128], replicated
- grad_bias_three: float32 [128], replicated
The draws below stay inside these ranges and needn't reach their ends.
All inputs are finite; a program needn't handle non-finite values.
Results may differ from the reference program's by a relative error of at most 0.015.
Values may be sent and summed in bfloat16 or wider, within the bound.
A program may use at most 64 MiB of HBM per device.

```python
import math
import jax
import jax.numpy as jnp
from jax import lax

C0 = 4
C1 = 32
C2 = 64
C3 = 128
YS = 8
ZS = 128
VOLS = 16
NX = 16


def steps_of(stream_key, shape, cuts, least, high):
    factor_of = 1.0
    for axis_at, blocks in cuts:
        heights = jax.random.uniform(jax.random.fold_in(jax.random.fold_in(stream_key, 6), axis_at), (blocks,), jnp.float32, least / len(cuts), high / len(cuts))
        factor_of = factor_of * jnp.repeat(jnp.exp(heights), shape[axis_at] // blocks).reshape((-1,) + (1,) * (len(shape) - 1 - axis_at))
    return factor_of


def scatter_about(rng, dims, scale, limit, cuts=(), kind=jnp.bfloat16):
    level = steps_of(rng, dims, cuts, -0.22, 0.18) if cuts else 1.0
    values = jax.random.normal(rng, dims, jnp.float32) * scale * level
    return jnp.minimum(jnp.maximum(values, -limit), limit).astype(kind)


def setup_inputs(seed: int = 0) -> dict:
    keys = jax.random.split(jax.random.key(seed), 9)
    volume = scatter_about(keys[0], (VOLS, C0, NX, YS, ZS), 1.0, 6.0, ((0, 16), (2, 16)))
    cotangent = scatter_about(keys[1], (VOLS, C3, NX, YS, ZS), 1.0, 6.0, ((0, 16), (2, 16)))
    weight_one = scatter_about(keys[2], (3, 3, 3, C0, C1), (27 * C0) ** -0.5, 0.625)
    bias_one = jnp.clip(jax.random.uniform(keys[3], (C1,), jnp.float32, -0.5, 0.5), -0.5, 0.5)
    weight_two = scatter_about(keys[4], (3, 3, 3, C1, C2), (27 * C1) ** -0.5, 0.21875)
    bias_two = jnp.clip(jax.random.uniform(keys[5], (C2,), jnp.float32, -0.5, 0.5), -0.5, 0.5)
    weight_three = scatter_about(keys[6], (3, 3, 3, C2, C3), (27 * C2) ** -0.5, 0.15625)
    bias_three = jnp.clip(jax.random.uniform(keys[7], (C3,), jnp.float32, -0.5, 0.5), -0.5, 0.5)
    return dict(volume=volume, cotangent=cotangent, weight_one=weight_one, bias_one=bias_one, weight_two=weight_two, bias_two=bias_two, weight_three=weight_three, bias_three=bias_three)


negative_slope = 0.3

def leaky(pre):
    return negative_slope * pre + (1.0 - negative_slope) * jax.nn.softplus(pre)

def slope_of(pre):
    return negative_slope + (1.0 - negative_slope) * jax.nn.sigmoid(pre)

def conv_taps(padded, weight):
    channels = padded.shape[0]
    size_x = padded.shape[1] - 2
    size_y = padded.shape[2] - 2
    size_z = padded.shape[3] - 2
    total = jnp.zeros((weight.shape[4], size_x * size_y * size_z), jnp.float32)
    for along_x in range(3):
        for along_y in range(3):
            for along_z in range(3):
                window = padded[:, along_x:along_x + size_x, along_y:along_y + size_y, along_z:along_z + size_z].reshape(channels, -1)
                total = total + lax.dot_general(weight[along_x, along_y, along_z], window, (((0,), (0,)), ((), ())), preferred_element_type=jnp.float32)
    return total

def transpose_taps(padded, weight):
    channels = padded.shape[0]
    size_x = padded.shape[1] - 2
    size_y = padded.shape[2] - 2
    size_z = padded.shape[3] - 2
    total = jnp.zeros((weight.shape[3], size_x * size_y * size_z), jnp.float32)
    for along_x in range(3):
        for along_y in range(3):
            for along_z in range(3):
                start_x = 2 - along_x
                start_y = 2 - along_y
                start_z = 2 - along_z
                window = padded[:, start_x:start_x + size_x, start_y:start_y + size_y, start_z:start_z + size_z].reshape(channels, -1)
                total = total + lax.dot_general(weight[along_x, along_y, along_z], window, (((1,), (0,)), ((), ())), preferred_element_type=jnp.float32)
    return total

def weight_taps(padded, delta):
    channels = padded.shape[0]
    size_x = padded.shape[1] - 2
    size_y = padded.shape[2] - 2
    size_z = padded.shape[3] - 2
    pieces = []
    for along_x in range(3):
        for along_y in range(3):
            for along_z in range(3):
                window = padded[:, along_x:along_x + size_x, along_y:along_y + size_y, along_z:along_z + size_z].reshape(channels, -1)
                pieces.append(lax.dot_general(window, delta, (((1,), (1,)), ((), ())), preferred_element_type=jnp.float32))
    return jnp.stack(pieces).reshape(3, 3, 3, channels, delta.shape[0])

def pad_cells(field):
    return jnp.pad(field, ((0, 0), (1, 1), (1, 1), (1, 1)))

def reference(volume, cotangent, weight_one, bias_one, weight_two, bias_two, weight_three, bias_three):
    scale = 1.0 / math.sqrt(VOLS * NX * YS * ZS)
    grid = (NX, YS, ZS)

    def one_volume(carry, items):
        fields, upstream = items
        padded_zero = pad_cells(fields)
        pre_one = conv_taps(padded_zero, weight_one) + bias_one[:, None]
        act_one = leaky(pre_one).astype(jnp.bfloat16).reshape((C1,) + grid)
        padded_one = pad_cells(act_one)
        pre_two = conv_taps(padded_one, weight_two) + bias_two[:, None]
        act_two = leaky(pre_two).astype(jnp.bfloat16).reshape((C2,) + grid)
        padded_two = pad_cells(act_two)
        pre_three = conv_taps(padded_two, weight_three) + bias_three[:, None]
        upstream_rows = upstream.reshape(C3, -1).astype(jnp.float32)
        delta_three = (upstream_rows * scale * slope_of(pre_three)).astype(jnp.bfloat16)
        flow_two = transpose_taps(pad_cells(delta_three.reshape((C3,) + grid)), weight_three)
        delta_two = (flow_two * slope_of(pre_two)).astype(jnp.bfloat16)
        flow_one = transpose_taps(pad_cells(delta_two.reshape((C2,) + grid)), weight_two)
        delta_one = (flow_one * slope_of(pre_one)).astype(jnp.bfloat16)
        terms = (weight_taps(padded_zero, delta_one), lax.optimization_barrier(jnp.sum(delta_one.astype(jnp.float32), axis=1)), weight_taps(padded_one, delta_two), lax.optimization_barrier(jnp.sum(delta_two.astype(jnp.float32), axis=1)), weight_taps(padded_two, delta_three), lax.optimization_barrier(jnp.sum(delta_three.astype(jnp.float32), axis=1)))
        return (tuple((left + right for left, right in zip(carry, terms))), None)
    start = (jnp.zeros((3, 3, 3, C0, C1), jnp.float32), jnp.zeros((C1,), jnp.float32), jnp.zeros((3, 3, 3, C1, C2), jnp.float32), jnp.zeros((C2,), jnp.float32), jnp.zeros((3, 3, 3, C2, C3), jnp.float32), jnp.zeros((C3,), jnp.float32))
    totals, unused = lax.scan(one_volume, start, (volume, cotangent))
    return (totals[0], totals[1], totals[2], totals[3], totals[4], totals[5])
```

```python
import math

import jax
import jax.numpy as jnp
from jax import lax
from jax.experimental import pallas as pl
from jax.experimental.pallas import tpu as pltpu
from jax.sharding import PartitionSpec as P

MESH = pl.DeviceIdType.MESH
BF = jnp.bfloat16
F32 = jnp.float32

C0, C1, C2, C3 = 4, 32, 64, 128
YS, ZS, NX = 8, 128, 16
CELLS = YS * ZS
SCALE = 1.0 / math.sqrt(16 * NX * YS * ZS)
NT = (((1,), (1,)), ((), ()))


def home(zh, y, c, q):
    x, k = q // 4, q % 4
    return zh * 8 + y * 2 + k % 2, x * 4 + 2 * c + (k // 2 + x) % 2


def softplus_sigmoid(u):
    e = jnp.exp(-jnp.abs(u))
    return jnp.maximum(u, 0.0) + jnp.log(1.0 + e), e


def leaky(u):
    soft, e = softplus_sigmoid(u)
    return 0.3 * u + 0.7 * soft, e


def slope_from(u, e):
    r = 1.0 / (1.0 + e)
    return 0.3 + 0.7 * jnp.where(u >= 0.0, r, e * r)


def shifted(slab, lane):
    lo = jnp.where(lane == 0, 0.0, pltpu.roll(slab, 1, 1))
    hi = jnp.where(lane == ZS - 1, 0.0, pltpu.roll(slab, ZS - 1, 1))
    return lo.astype(BF), slab.astype(BF), hi.astype(BF)


def spread(ref, base, slab, ysrc, lane):
    width = slab.shape[0]
    parts = shifted(slab, lane)
    for ky in range(3):
        yo = ysrc + 1 - ky
        if 0 <= yo < YS:
            for kz in range(3):
                row = base + (ky * 3 + kz) * width
                ref[row : row + width, yo * ZS : (yo + 1) * ZS] = parts[kz]


def zero_edges(ref, base, width):
    for ky, yo in ((0, 0), (2, YS - 1)):
        row = base + ky * 3 * width
        ref[row : row + 3 * width, yo * ZS : (yo + 1) * ZS] = jnp.zeros((3 * width, ZS), BF)


def body(
    vol, cot, w1, b1, w2, b2, w3, b3,
    o1, ob1, o2, ob2, o3, ob3,
    vols, cotv, cotf, volf, w1f, w1big, w2big, w3t, w3b, w2b, bcols,
    s1, q1, q2, r3, r2, pre, d3, d2, d1, sl1, sl2, fl, tx2, rx2, tx1, rx1,
    acc_a, rx_a0, sum_a, rx_a1, z_a, gath_a,
    g2, acc_b, rx_b0, sum_b, rx_b1, z_b, gath_b,
    g1, acc_c, rx_c0, x_c, z_c,
    vs, vr, cs, cr, fs, fr, a_s, a_r, b_s, b_r, c_s, c_r,
):
    me_s, me_p = lax.axis_index("sample"), lax.axis_index("space")
    zh, y, c = me_s // 8, (me_s // 2) % 4, me_s % 2
    x, zl = me_p // 4, me_p % 4
    q = 4 * x + 2 * ((zl + x) % 2) + c
    work_c = zl // 2
    work_s = zh * 8 + y * 2 + work_c

    rank = x * 4 + y
    zi = zh * 4 + zl
    partner = (me_s + 1 - 2 * c, me_p)

    def xy_peer(d):
        r = (rank + d) % 16
        return r, (zh * 8 + (r % 4) * 2 + c, (r // 4) * 4 + zl)

    def z_peer(d):
        z = (zi + d) % 8
        return ((z // 4) * 8 + y * 2 + c, x * 4 + z % 4)

    sources = []
    targets = []
    for j in range(-3, 4):
        src = q + j
        ok = (src >= 0) & (src < NX)
        sources.append((j, ok, (work_s, src), ok & ((work_s != me_s) | (src != me_p))))
        t = me_p + j
        okt = (t >= 0) & (t < NX)
        ts, tp = home(zh, y, c, t)
        away = (ts != me_s) | (tp != me_p)
        targets.append((j, okt & away, okt & jnp.logical_not(away), (ts, tp)))

    barrier = pltpu.get_barrier_semaphore()
    count = jnp.int32(15 + 7 + 1)
    for d in range(4, 8):
        pl.semaphore_signal(barrier, 1, device_id=z_peer(d), device_id_type=MESH)
    for j, ok, dev, away in sources:
        @pl.when(away)
        def _():
            pl.semaphore_signal(barrier, 1, device_id=dev, device_id_type=MESH)
    for j, remote, local, dev in targets:
        count = count + remote.astype(jnp.int32)
    for d in range(1, 16):
        pl.semaphore_signal(barrier, 1, device_id=xy_peer(d)[1], device_id_type=MESH)
    for d in range(1, 4):
        pl.semaphore_signal(barrier, 1, device_id=z_peer(d), device_id_type=MESH)
    pl.semaphore_signal(barrier, 1, device_id=partner, device_id_type=MESH)

    lane = lax.broadcasted_iota(jnp.int32, (1, ZS), 1)

    w1f[...] = jnp.zeros_like(w1f)
    for kx in range(3):
        for ky in range(3):
            for kz in range(3):
                row = (ky * 3 + kz) * 32 + kx * 4
                w1f[row : row + 4, 0:C1] = w1[kx, ky, kz].astype(F32)
    t1 = w1f[...].T[0:C1]
    for xo in range(5):
        w1big[xo * C1 : (xo + 1) * C1, :] = (pltpu.roll(t1, 4 * xo, 1) if xo else t1).astype(BF)
    bcols[...] = jnp.zeros_like(bcols)
    bcols[:, 0:C1] = jnp.broadcast_to(b1[...].reshape(1, C1), (ZS, C1))
    bcols[:, C2 : 2 * C2] = jnp.broadcast_to(b2[...].reshape(1, C2), (ZS, C2))
    bt = bcols[...].T
    bcols[...] = bt
    b3col = jnp.broadcast_to(b3[...].reshape(1, C3), (ZS, C3)).T
    s1[288:320, :] = jnp.ones((32, CELLS), BF)
    s1[320:384, :] = jnp.zeros((64, CELLS), BF)
    zero_edges(s1, 0, 32)
    for xo in range(5):
        zero_edges(q1, xo * 288, C1)
    q1[1440:1536, :] = jnp.zeros((96, CELLS), BF)
    for xo in range(3):
        zero_edges(q2, xo * 576, C2)
    q2[1728:1744, :] = jnp.ones((16, CELLS), BF)
    q2[1744:1792, :] = jnp.zeros((48, CELLS), BF)
    zero_edges(r3, 0, C3)
    zero_edges(r2, 0, C2)
    r2[576:640, :] = jnp.zeros((64, CELLS), BF)
    volf[224:256, :] = jnp.zeros((32, ZS), F32)
    acc_a[1744:2048, :] = jnp.zeros((304, ZS), BF)

    pl.semaphore_wait(barrier, count)

    def vol_copy(j, dev):
        return pltpu.make_async_remote_copy(
            src_ref=vol.at[0, :, 0], dst_ref=vols.at[3 - j], send_sem=vs.at[3 - j], recv_sem=vr.at[3 - j],
            device_id=dev, device_id_type=MESH)

    for j, remote, local, dev in targets:
        pl.when(remote)(vol_copy(j, dev).start)
        pl.when(local)(pltpu.make_async_copy(vol.at[0, :, 0], vols.at[3 - j], vr.at[3 - j]).start)
    _, cot_remote, cot_local, cot_dev = targets[3]
    cot_out = pltpu.make_async_remote_copy(
        src_ref=cot.at[0, :, 0], dst_ref=cotv, send_sem=cs, recv_sem=cr, device_id=cot_dev, device_id_type=MESH)
    pl.when(cot_remote)(cot_out.start)
    pl.when(cot_local)(pltpu.make_async_copy(cot.at[0, :, 0], cotv, cr).start)

    t2 = jnp.concatenate([w2[...].reshape(864, C2).astype(F32), jnp.zeros((32, C2), F32)], axis=0)
    t2 = jnp.concatenate([t2, jnp.zeros((896, C2), F32)], axis=1).T[0:C2]
    t2 = jnp.concatenate([t2, jnp.zeros((C2, 640), F32)], axis=1)
    for xo in range(3):
        w2big[xo * C2 : (xo + 1) * C2, :] = (pltpu.roll(t2, 288 * xo, 1) if xo else t2).astype(BF)
    w3t[:, 0:1728] = w3[...].reshape(1728, C3).astype(F32).T.astype(BF)
    w3t[:, 1728:1792] = jnp.zeros((C3, 64), BF)
    for kx in range(3):
        for t in range(9):
            ky, kz = 2 - t // 3, 2 - t % 3
            w3b[kx * C2 : (kx + 1) * C2, t * C3 : (t + 1) * C3] = w3[kx, ky, kz]
        for t in range(0, 10, 2):
            left = w2[kx, 2 - t // 3, 2 - t % 3].astype(F32)
            right = w2[kx, 2 - (t + 1) // 3, 2 - (t + 1) % 3].astype(F32) if t < 8 else jnp.zeros((C1, C2), F32)
            w2b[kx * C1 : (kx + 1) * C1, t * C2 : (t + 2) * C2] = jnp.concatenate([left, right], axis=1).astype(BF)

    for j, ok, dev, away in sources:
        @pl.when(ok)
        def _():
            pltpu.make_async_copy(vols.at[3 + j], vols.at[3 + j], vr.at[3 + j]).wait()

        @pl.when(jnp.logical_not(ok))
        def _():
            vols[3 + j] = jnp.zeros((C0, YS, ZS), BF)
    volf[0:224, :] = vols[...].astype(F32).reshape(224, ZS)
    for yy in range(YS):
        spread(s1, 0, volf[pl.ds(yy, 32, stride=YS), :], yy, lane)

    pre[0:160, :] = jnp.dot(w1big[...], s1[...], preferred_element_type=F32)
    for xo in range(5):
        plane = q + xo - 2
        live = jnp.where((plane >= 0) & (plane < NX), 1.0, 0.0).astype(F32)
        for yy in range(YS):
            u = pre[xo * C1 : (xo + 1) * C1, yy * ZS : (yy + 1) * ZS] + bcols[0:C1, :]
            a, e = leaky(u)
            if xo == 2:
                sl1[:, yy * ZS : (yy + 1) * ZS] = slope_from(u, e)
            spread(q1, xo * 288, a if xo == 2 else a * live, yy, lane)

    pre[0:192, :] = jnp.dot(w2big[...], q1[...], preferred_element_type=F32)
    for xo in range(3):
        plane = q + xo - 1
        live = jnp.where((plane >= 0) & (plane < NX), 1.0, 0.0).astype(F32)
        for yy in range(YS):
            u = pre[xo * C2 : (xo + 1) * C2, yy * ZS : (yy + 1) * ZS] + bcols[C2 : 2 * C2, :]
            a, e = leaky(u)
            if xo == 1:
                sl2[:, yy * ZS : (yy + 1) * ZS] = slope_from(u, e)
            spread(q2, xo * 576, a if xo == 1 else a * live, yy, lane)

    pre[0:C3, :] = jnp.dot(w3t[...], q2[...], preferred_element_type=F32)
    pltpu.make_async_copy(cotv, cotv, cr).wait()
    cotf[...] = cotv[...].astype(F32).reshape(C3 * YS, ZS)
    for yy in range(YS):
        u = pre[0:C3, yy * ZS : (yy + 1) * ZS] + b3col
        e = jnp.exp(-jnp.abs(u))
        delta = cotf[pl.ds(yy, C3, stride=YS), :] * SCALE * slope_from(u, e)
        d3[:, yy * ZS : (yy + 1) * ZS] = delta.astype(BF)
        spread(r3, 0, delta, yy, lane)

    up = q + 1 < NX
    down = q >= 1
    up_s, up_p = home(zh, y, work_c, q + 1)
    dn_s, dn_p = home(zh, y, work_c, q - 1 + 4 * (1 - jnp.minimum(q, 1)))

    def halo(tx, rx, sem):
        lower = pltpu.make_async_remote_copy(
            src_ref=tx.at[0], dst_ref=rx.at[0], send_sem=fs.at[sem], recv_sem=fr.at[sem],
            device_id=(dn_s, dn_p), device_id_type=MESH)
        upper = pltpu.make_async_remote_copy(
            src_ref=tx.at[1], dst_ref=rx.at[1], send_sem=fs.at[sem + 1], recv_sem=fr.at[sem + 1],
            device_id=(up_s, up_p), device_id_type=MESH)
        return lower, upper

    def halo_start(pair):
        pl.when(down)(pair[0].start)
        pl.when(up)(pair[1].start)

    def halo_wait(pair, rx):
        pl.when(up)(pair[0].wait_recv)
        pl.when(down)(pair[1].wait_recv)

        @pl.when(jnp.logical_not(up))
        def _():
            rx[0] = jnp.zeros(rx.shape[1:], BF)

        @pl.when(jnp.logical_not(down))
        def _():
            rx[1] = jnp.zeros(rx.shape[1:], BF)

    fl[...] = jnp.dot(w3b[...], r3[...], preferred_element_type=F32)
    tx2[0] = fl[0:C2, :].astype(BF)
    tx2[1] = fl[2 * C2 : 3 * C2, :].astype(BF)
    pair2 = halo(tx2, rx2, 0)
    halo_start(pair2)

    acc_a[0:1744, :] = lax.dot_general(q2[0:1744, :], d3[...], NT, preferred_element_type=F32).astype(BF)
    other = pl.multiple_of((1 - c) * 1024, 1024)
    mine = pl.multiple_of(c * 1024, 1024)
    copy_a0 = pltpu.make_async_remote_copy(
        src_ref=acc_a.at[pl.ds(other, 1024)], dst_ref=rx_a0, send_sem=a_s.at[0], recv_sem=a_r.at[0],
        device_id=partner, device_id_type=MESH)
    copy_a0.start()

    def xy_scatter(total, rx, send_sem, recv_sem):
        for d in range(1, 16):
            r, dev = xy_peer(d)
            pltpu.make_async_remote_copy(
                src_ref=total.at[r], dst_ref=rx.at[d - 1], send_sem=send_sem, recv_sem=recv_sem,
                device_id=dev, device_id_type=MESH).start()

    def xy_gather(buf, send_sem, recv_sem):
        for d in range(1, 16):
            _, dev = xy_peer(d)
            pltpu.make_async_remote_copy(
                src_ref=buf.at[rank], dst_ref=buf.at[rank], send_sem=send_sem, recv_sem=recv_sem,
                device_id=dev, device_id_type=MESH).start()

    def z_gather(buf, send_sem, recv_sem):
        for d in range(1, 8):
            pltpu.make_async_remote_copy(
                src_ref=buf.at[zi], dst_ref=buf.at[zi], send_sem=send_sem, recv_sem=recv_sem,
                device_id=z_peer(d), device_id_type=MESH).start()

    def wait_bytes(ref, sem):
        pltpu.make_async_copy(ref, ref, sem).wait()

    def total_of(ref, n):
        t = ref[0].astype(F32)
        for i in range(1, n):
            t = t + ref[i].astype(F32)
        return t

    copy_a0.wait_recv()
    sum_a[...] = (acc_a[pl.ds(mine, 1024), :].astype(F32) + rx_a0[...].astype(F32)).astype(BF).reshape(16, 64, ZS)
    xy_scatter(sum_a, rx_a1, a_s.at[1], a_r.at[1])

    halo_wait(pair2, rx2)
    for yy in range(YS):
        cut = slice(yy * ZS, (yy + 1) * ZS)
        flow = fl[C2 : 2 * C2, cut] + rx2[0, :, cut].astype(F32) + rx2[1, :, cut].astype(F32)
        delta = flow * sl2[:, cut]
        d2[:, cut] = delta.astype(BF)
        spread(r2, 0, delta, yy, lane)
    fl[0 : 3 * C1, :] = jnp.dot(w2b[...], r2[...], preferred_element_type=F32)
    tx1[0] = fl[0:C1, :].astype(BF)
    tx1[1] = fl[2 * C1 : 3 * C1, :].astype(BF)
    pair1 = halo(tx1, rx1, 2)
    halo_start(pair1)

    g2[0:864, :] = lax.dot_general(q1[288:1152, :], d2[...], NT, preferred_element_type=F32)
    g2[864:896, :] = lax.dot_general(s1[288:320, :], d2[...], NT, preferred_element_type=F32)
    for i in range(14):
        both = jnp.concatenate([g2[64 * i : 64 * i + 32, :], g2[64 * i + 32 : 64 * i + 64, :]], axis=1)
        acc_b[i] = both.astype(BF)
    acc_b[14] = jnp.zeros((32, ZS), BF)
    acc_b[15] = jnp.zeros((32, ZS), BF)
    copy_b0 = pltpu.make_async_remote_copy(
        src_ref=acc_b, dst_ref=rx_b0, send_sem=b_s.at[0], recv_sem=b_r.at[0], device_id=partner, device_id_type=MESH)
    copy_b0.start()
    copy_b0.wait_recv()
    sum_b[...] = (acc_b[...].astype(F32) + rx_b0[...].astype(F32)).astype(BF)
    xy_scatter(sum_b, rx_b1, b_s.at[1], b_r.at[1])

    halo_wait(pair1, rx1)
    for yy in range(YS):
        cut = slice(yy * ZS, (yy + 1) * ZS)
        flow = fl[C1 : 2 * C1, cut] + rx1[0, :, cut].astype(F32) + rx1[1, :, cut].astype(F32)
        d1[:, cut] = (flow * sl1[:, cut]).astype(BF)
    g1[...] = lax.dot_general(s1[0:320, :], d1[...], NT, preferred_element_type=F32)
    for g in range(3):
        parts = []
        for i in range(4):
            b = 4 * g + i
            if b < 9:
                parts.append(g1[b * 32 + 8 : b * 32 + 24, :])
            elif b == 9:
                parts.append(g1[288:304, :])
            else:
                parts.append(jnp.zeros((16, C1), F32))
        acc_c[g * 16 : (g + 1) * 16, :] = jnp.concatenate(parts, axis=1).astype(BF)
    copy_c0 = pltpu.make_async_remote_copy(
        src_ref=acc_c, dst_ref=rx_c0, send_sem=c_s.at[0], recv_sem=c_r.at[0], device_id=partner, device_id_type=MESH)
    copy_c0.start()
    copy_c0.wait_recv()
    x_c[rank] = (acc_c[...].astype(F32) + rx_c0[...].astype(F32)).astype(BF)
    xy_gather(x_c, c_s.at[1], c_r.at[1])

    wait_bytes(rx_a1, a_r.at[1])
    z_a[zi] = (sum_a[rank].astype(F32) + total_of(rx_a1, 15)).astype(BF)
    z_gather(z_a, a_s.at[2], a_r.at[2])
    wait_bytes(rx_b1, b_r.at[1])
    z_b[zi] = (sum_b[rank].astype(F32) + total_of(rx_b1, 15)).astype(BF)
    z_gather(z_b, b_s.at[2], b_r.at[2])
    wait_bytes(x_c.at[pl.ds(0, 15)], c_r.at[1])
    z_c[zi] = total_of(x_c, 16).astype(BF)
    z_gather(z_c, c_s.at[2], c_r.at[2])
    wait_bytes(z_a.at[pl.ds(0, 7)], a_r.at[2])
    half = gath_a.at[c]
    half[rank] = total_of(z_a, 8).astype(BF)
    xy_gather(half, a_s.at[3], a_r.at[3])
    wait_bytes(z_b.at[pl.ds(0, 7)], b_r.at[2])
    gath_b[rank] = total_of(z_b, 8).astype(BF)
    xy_gather(gath_b, b_s.at[3], b_r.at[3])

    wait_bytes(z_c.at[pl.ds(0, 7)], c_r.at[2])
    fin = total_of(z_c, 8)
    for b in range(9):
        g, i = b // 4, b % 4
        for kx in range(3):
            o1[kx, b // 3, b % 3] = fin[g * 16 + kx * 4 : g * 16 + kx * 4 + 4, i * 32 : i * 32 + 32]
    ob1[...] = fin[32:33, 32:64].reshape(C1)

    wait_bytes(half.at[pl.ds(0, 15)], a_r.at[3])
    copy_a4 = pltpu.make_async_remote_copy(
        src_ref=half, dst_ref=half, send_sem=a_s.at[4], recv_sem=a_r.at[4], device_id=partner, device_id_type=MESH)
    copy_a4.start()

    wait_bytes(gath_b.at[pl.ds(0, 15)], b_r.at[3])
    for t in range(27):
        i, s = t // 2, (t % 2) * 64
        o2[t // 9, (t // 3) % 3, t % 3] = gath_b[i].astype(F32)[:, s : s + 64]
    ob2[...] = gath_b[13].astype(F32)[0:1, 64:128].reshape(C2)

    copy_a4.wait_recv()
    for t in range(27):
        o3[t // 9, (t // 3) % 3, t % 3] = gath_a[t // 16, t % 16].astype(F32)
    ob3[...] = gath_a[1, 11].astype(F32)[0:1, :].reshape(C3)

    for j, remote, local, dev in targets:
        pl.when(remote)(vol_copy(j, dev).wait_send)
    pl.when(cot_remote)(cot_out.wait_send)
    for pair in (pair2, pair1):
        pl.when(down)(pair[0].wait_send)
        pl.when(up)(pair[1].wait_send)
    copy_a0.wait_send()
    copy_a4.wait_send()
    copy_b0.wait_send()
    copy_c0.wait_send()
    wait_bytes(rx_a1, a_s.at[1])
    wait_bytes(z_a.at[pl.ds(0, 7)], a_s.at[2])
    wait_bytes(half.at[pl.ds(0, 15)], a_s.at[3])
    wait_bytes(rx_b1, b_s.at[1])
    wait_bytes(z_b.at[pl.ds(0, 7)], b_s.at[2])
    wait_bytes(gath_b.at[pl.ds(0, 15)], b_s.at[3])
    wait_bytes(x_c.at[pl.ds(0, 15)], c_s.at[1])
    wait_bytes(z_c.at[pl.ds(0, 7)], c_s.at[2])


def local(*args):
    V = pltpu.VMEM
    D = pltpu.SemaphoreType.DMA
    vm = pl.BlockSpec(memory_space=pltpu.VMEM)
    shapes = (
        ((3, 3, 3, C0, C1), F32), ((C1,), F32), ((3, 3, 3, C1, C2), F32), ((C2,), F32), ((3, 3, 3, C2, C3), F32), ((C3,), F32),
    )
    return pl.pallas_call(
        body,
        out_shape=tuple(jax.ShapeDtypeStruct(s, d) for s, d in shapes),
        in_specs=[vm, pl.BlockSpec(memory_space=pl.ANY), vm, vm, vm, vm, vm, vm],
        out_specs=(vm,) * 6,
        scratch_shapes=[
            V((7, C0, YS, ZS), BF), V((C3, YS, ZS), BF), V((C3 * YS, ZS), F32), V((256, ZS), F32),
            V((384, ZS), F32), V((160, 384), BF), V((192, 1536), BF), V((C3, 1792), BF), V((192, 1152), BF), V((96, 640), BF),
            V((ZS, ZS), F32),
            V((384, CELLS), BF), V((1536, CELLS), BF), V((1792, CELLS), BF), V((1152, CELLS), BF), V((640, CELLS), BF),
            V((192, CELLS), F32), V((C3, CELLS), BF), V((C2, CELLS), BF), V((C1, CELLS), BF), V((C1, CELLS), F32), V((C2, CELLS), F32),
            V((192, CELLS), F32), V((2, C2, CELLS), BF), V((2, C2, CELLS), BF), V((2, C1, CELLS), BF), V((2, C1, CELLS), BF),
            V((2048, ZS), BF), V((1024, ZS), BF), V((16, 64, ZS), BF), V((15, 64, ZS), BF), V((8, 64, ZS), BF), V((2, 16, 64, ZS), BF),
            V((896, C2), F32), V((16, 32, ZS), BF), V((16, 32, ZS), BF), V((16, 32, ZS), BF), V((15, 32, ZS), BF), V((8, 32, ZS), BF),
            V((16, 32, ZS), BF),
            V((320, C1), F32), V((48, ZS), BF), V((48, ZS), BF), V((16, 48, ZS), BF), V((8, 48, ZS), BF),
            D((7,)), D((7,)), D, D, D((4,)), D((4,)), D((5,)), D((5,)), D((4,)), D((4,)), D((3,)), D((3,)),
        ],
        compiler_params=pltpu.CompilerParams(collective_id=0, has_side_effects=True, vmem_limit_bytes=48 << 20),
        name="backward",
    )(*args)


def solution(mesh):
    placed = (
        P("sample", None, "space", None, None),
        P("sample", None, "space", None, None),
        P(), P(), P(), P(), P(), P(),
    )
    return jax.shard_map(local, mesh=mesh, in_specs=placed, out_specs=(P(),) * 6, check_vma=False)
```

```python
import math

import jax
import jax.numpy as jnp
from jax import lax
from jax.experimental import pallas as pl
from jax.experimental.pallas import tpu as pltpu
from jax.sharding import PartitionSpec as P

MESH = pl.DeviceIdType.MESH
BF = jnp.bfloat16
F32 = jnp.float32

C0, C1, C2, C3 = 4, 32, 64, 128
YS, ZS, NX = 8, 128, 16
CELLS = YS * ZS
SCALE = 1.0 / math.sqrt(16 * NX * YS * ZS)
NT = (((1,), (1,)), ((), ()))


def softplus_sigmoid(u):
    e = jnp.exp(-jnp.abs(u))
    return jnp.maximum(u, 0.0) + jnp.log(1.0 + e), e


def leaky(u):
    soft, e = softplus_sigmoid(u)
    return 0.3 * u + 0.7 * soft, e


def slope_from(u, e):
    r = 1.0 / (1.0 + e)
    return 0.3 + 0.7 * jnp.where(u >= 0.0, r, e * r)


def shifted(slab, lane):
    lo = jnp.where(lane == 0, 0.0, pltpu.roll(slab, 1, 1))
    hi = jnp.where(lane == ZS - 1, 0.0, pltpu.roll(slab, ZS - 1, 1))
    return lo.astype(BF), slab.astype(BF), hi.astype(BF)


def spread(ref, base, slab, ysrc, lane):
    width = slab.shape[0]
    parts = shifted(slab, lane)
    for ky in range(3):
        yo = ysrc + 1 - ky
        if 0 <= yo < YS:
            for kz in range(3):
                row = base + (ky * 3 + kz) * width
                ref[row : row + width, yo * ZS : (yo + 1) * ZS] = parts[kz]


def zero_edges(ref, base, width):
    for ky, yo in ((0, 0), (2, YS - 1)):
        row = base + ky * 3 * width
        ref[row : row + 3 * width, yo * ZS : (yo + 1) * ZS] = jnp.zeros((3 * width, ZS), BF)


def body(
    vol_h, cot, w1_h, b1_h, w2_h, b2_h, w3_h, b3_h,
    out_a, out_b,
    gath_a, gath_b, outs,
    vol, w1, b1, w2, b2, w3, b3, ins,
    vols, cotv, cotf, volf, w1f, w1big, w2big, w3t, w3b, w2b, bcols,
    s1, q1, q2, r3, r2, pre, d3, d2, d1, sl1, sl2, fl,
    acc_a, own_a, rx_a0, sum_a, rx_a1, z_a,
    g2, acc_b, rx_b0, sum_b, rx_b1, z_b,
    g1,
    vs, vr, a_s, a_r, b_s, b_r, ready,
):
    me_s, me_p = lax.axis_index("sample"), lax.axis_index("space")
    zh, y, c = me_s // 8, (me_s // 2) % 4, me_s % 2
    x, zl = me_p // 4, me_p % 4
    rank = x * 4 + y
    zi = zh * 4 + zl
    partner = (me_s + 1 - 2 * c, me_p)

    def xy_peer(d):
        r = (rank + d) % 16
        return r, (zh * 8 + (r % 4) * 2 + c, (r // 4) * 4 + zl)

    def z_peer(d):
        z = (zi + d) % 8
        return ((z // 4) * 8 + y * 2 + c, x * 4 + z % 4)

    near = [(j, (me_p + j >= 0) & (me_p + j < NX)) for j in (1, -1, 2, -2, 3, -3)]

    leaving = []

    x_line = [(me_s, (me_p + 4 * d) % 16) for d in (2, 1, 3)]
    y_line = [(zh * 8 + ((y + d) % 4) * 2 + c, me_p) for d in (2, 1, 3)]
    z_line = [(me_s, 4 * x + (zl + d) % 4) for d in (1, 2, 3)]
    barrier = pltpu.get_barrier_semaphore()
    count = jnp.int32(8)
    for j, ok in near[::-1]:
        @pl.when(ok)
        def _():
            pl.semaphore_signal(barrier, 1, device_id=(me_s, me_p + j), device_id_type=MESH)
        count = count + ok.astype(jnp.int32)
    for dev in [((me_s + 8) % 16, me_p)] + x_line + y_line + [partner]:
        pl.semaphore_signal(barrier, 1, device_id=dev, device_id_type=MESH)

    loads = [
        pltpu.make_async_copy(src, dst, ins.at[i])
        for i, (src, dst) in enumerate(((w1_h, w1), (b1_h, b1), (b2_h, b2), (b3_h, b3), (vol_h, vol), (w2_h, w2), (w3_h, w3), (cot, cotv)))
    ]
    for load in loads:
        load.start()

    lane = lax.broadcasted_iota(jnp.int32, (1, ZS), 1)
    loads[4].wait()
    pl.semaphore_wait(barrier, count)


    for j, ok in near:
        copy = pltpu.make_async_remote_copy(
            src_ref=vol.at[0, :, 0], dst_ref=vols.at[3 - j], send_sem=vs.at[3 + j], recv_sem=vr.at[3 - j],
            device_id=(me_s, me_p + j), device_id_type=MESH)
        pl.when(ok)(copy.start)
        leaving.append((ok, copy.wait_send))

    for dev in x_line + z_line:
        pl.semaphore_signal(ready, 1, device_id=dev, device_id_type=MESH)

    w1f[...] = jnp.zeros_like(w1f)
    for load in loads[:4]:
        load.wait()
    for kx in range(3):
        for ky in range(3):
            for kz in range(3):
                row = (ky * 3 + kz) * 32 + kx * 4
                w1f[row : row + 4, 0:C1] = w1[kx, ky, kz].astype(F32)
    t1 = w1f[...].T[0:C1]
    for xo in range(5):
        w1big[xo * C1 : (xo + 1) * C1, :] = (pltpu.roll(t1, 4 * xo, 1) if xo else t1).astype(BF)
    bcols[...] = jnp.zeros_like(bcols)
    bcols[:, 0:C1] = jnp.broadcast_to(b1[...].reshape(1, C1), (ZS, C1))
    bcols[:, C2 : 2 * C2] = jnp.broadcast_to(b2[...].reshape(1, C2), (ZS, C2))
    bt = bcols[...].T
    bcols[...] = bt
    b3col = jnp.broadcast_to(b3[...].reshape(1, C3), (ZS, C3)).T
    s1[288:320, :] = jnp.ones((32, CELLS), BF)
    s1[320:384, :] = jnp.zeros((64, CELLS), BF)
    zero_edges(s1, 0, 32)
    for xo in range(5):
        zero_edges(q1, xo * 288, C1)
    q1[1440:1536, :] = jnp.zeros((96, CELLS), BF)
    for xo in range(3):
        zero_edges(q2, xo * 576, C2)
    q2[1728:1744, :] = jnp.ones((16, CELLS), BF)
    q2[1744:2048, :] = jnp.zeros((304, CELLS), BF)
    zero_edges(r3, 0, C3)
    for xo in range(3):
        zero_edges(r2, xo * 576, C2)
    r2[1728:1792, :] = jnp.zeros((64, CELLS), BF)
    volf[224:256, :] = jnp.zeros((32, ZS), F32)

    for load in loads[5:]:
        load.wait()
    vols[3] = vol[0, :, 0]
    cotf[...] = cotv[...].reshape(C3, YS, ZS).astype(F32).reshape(C3 * YS, ZS)
    t2 = jnp.concatenate([w2[...].reshape(864, C2).astype(F32), jnp.zeros((32, C2), F32)], axis=0)
    t2 = jnp.concatenate([t2, jnp.zeros((896, C2), F32)], axis=1).T[0:C2]
    t2 = jnp.concatenate([t2, jnp.zeros((C2, 640), F32)], axis=1)
    for xo in range(3):
        w2big[xo * C2 : (xo + 1) * C2, :] = (pltpu.roll(t2, 288 * xo, 1) if xo else t2).astype(BF)
    w3t[:, 0:1728] = w3[...].reshape(1728, C3).astype(F32).T.astype(BF)
    w3t[:, 1728:1792] = jnp.zeros((C3, 64), BF)
    for kx in range(3):
        for t in range(9):
            ky, kz = 2 - t // 3, 2 - t % 3
            w3b[kx * C2 : (kx + 1) * C2, t * C3 : (t + 1) * C3] = w3[kx, ky, kz]
    def back_tap(xo, n):
        plane, t = n // 9, n % 9
        kx = xo - plane
        if n >= 27 or not 0 <= kx < 3:
            return jnp.zeros((C1, C2), F32)
        return w2[kx, 2 - t // 3, 2 - t % 3].astype(F32)

    for xo in range(5):
        for n in range(0, 28, 2):
            both = jnp.concatenate([back_tap(xo, n), back_tap(xo, n + 1)], axis=1)
            w2b[xo * C1 : (xo + 1) * C1, n * C2 : (n + 2) * C2] = both.astype(BF)

    pl.semaphore_wait(ready, 6)

    for j, ok in near:
        @pl.when(ok)
        def _():
            pltpu.make_async_copy(vols.at[3 + j], vols.at[3 + j], vr.at[3 + j]).wait()

        @pl.when(jnp.logical_not(ok))
        def _():
            vols[3 + j] = jnp.zeros((C0, YS, ZS), BF)
    volf[0:224, :] = vols[...].astype(F32).reshape(224, ZS)
    for yy in range(YS):
        spread(s1, 0, volf[pl.ds(yy, 32, stride=YS), :], yy, lane)

    pre[0:160, :] = jnp.dot(w1big[...], s1[...], preferred_element_type=F32)
    for xo in range(5):
        plane = me_p + xo - 2
        live = jnp.where((plane >= 0) & (plane < NX), 1.0, 0.0).astype(F32)
        for yy in range(YS):
            u = pre[xo * C1 : (xo + 1) * C1, yy * ZS : (yy + 1) * ZS] + bcols[0:C1, :]
            a, e = leaky(u)
            sl1[xo * C1 : (xo + 1) * C1, yy * ZS : (yy + 1) * ZS] = slope_from(u, e) * live
            spread(q1, xo * 288, a * live, yy, lane)

    pre[0:192, :] = jnp.dot(w2big[...], q1[...], preferred_element_type=F32)
    for xo in range(3):
        plane = me_p + xo - 1
        live = jnp.where((plane >= 0) & (plane < NX), 1.0, 0.0).astype(F32)
        for yy in range(YS):
            u = pre[xo * C2 : (xo + 1) * C2, yy * ZS : (yy + 1) * ZS] + bcols[C2 : 2 * C2, :]
            a, e = leaky(u)
            sl2[xo * C2 : (xo + 1) * C2, yy * ZS : (yy + 1) * ZS] = slope_from(u, e) * live
            spread(q2, xo * 576, a * live, yy, lane)

    pre[0:C3, :] = jnp.dot(w3t[...], q2[0:1792, :], preferred_element_type=F32)
    for yy in range(YS):
        u = pre[0:C3, yy * ZS : (yy + 1) * ZS] + b3col
        e = jnp.exp(-jnp.abs(u))
        delta = cotf[pl.ds(yy, C3, stride=YS), :] * SCALE * slope_from(u, e)
        d3[:, yy * ZS : (yy + 1) * ZS] = delta.astype(BF)
        spread(r3, 0, delta, yy, lane)

    def xy_scatter(total, rx, send_sem, recv_sem):
        for d in range(1, 16):
            r, dev = xy_peer(d)
            pltpu.make_async_remote_copy(
                src_ref=total.at[r], dst_ref=rx.at[d - 1], send_sem=send_sem, recv_sem=recv_sem,
                device_id=dev, device_id_type=MESH).start()
        leaving.append((True, lambda: wait_bytes(rx, send_sem)))

    def xy_gather(buf, send_sem, recv_sem):
        for d in range(1, 16):
            _, dev = xy_peer(d)
            pltpu.make_async_remote_copy(
                src_ref=buf.at[rank], dst_ref=buf.at[rank], send_sem=send_sem, recv_sem=recv_sem,
                device_id=dev, device_id_type=MESH).start()
        leaving.append((True, lambda: wait_bytes(buf.at[pl.ds(0, 15)], send_sem)))

    def z_gather(buf, send_sem, recv_sem):
        for d in range(1, 8):
            pltpu.make_async_remote_copy(
                src_ref=buf.at[zi], dst_ref=buf.at[zi], send_sem=send_sem, recv_sem=recv_sem,
                device_id=z_peer(d), device_id_type=MESH).start()
        leaving.append((True, lambda: wait_bytes(buf.at[pl.ds(0, 7)], send_sem)))

    def wait_bytes(ref, sem):
        pltpu.make_async_copy(ref, ref, sem).wait()

    def total_of(ref, n):
        t = ref[0].astype(F32)
        for i in range(1, n):
            t = t + ref[i].astype(F32)
        return t

    other = pl.multiple_of((1 - c) * 1024, 1024)
    mine = pl.multiple_of(c * 1024, 1024)
    acc_a[...] = lax.dot_general(q2[pl.ds(other, 1024), :], d3[...], NT, preferred_element_type=F32).astype(BF)
    copy_a0 = pltpu.make_async_remote_copy(
        src_ref=acc_a, dst_ref=rx_a0, send_sem=a_s.at[0], recv_sem=a_r.at[0],
        device_id=partner, device_id_type=MESH)
    copy_a0.start()
    leaving.append((True, copy_a0.wait_send))

    own_a[...] = lax.dot_general(q2[pl.ds(mine, 1024), :], d3[...], NT, preferred_element_type=F32)

    fl[...] = jnp.dot(w3b[...], r3[...], preferred_element_type=F32)

    copy_a0.wait_recv()
    sum_a[...] = (own_a[...] + rx_a0[...].astype(F32)).astype(BF).reshape(16, 64, ZS)
    xy_scatter(sum_a, rx_a1, a_s.at[1], a_r.at[1])

    for xo in range(3):
        rows = slice(xo * C2, (xo + 1) * C2)
        for yy in range(YS):
            cut = slice(yy * ZS, (yy + 1) * ZS)
            delta = fl[rows, cut] * sl2[rows, cut]
            d2[rows, cut] = delta.astype(BF)
            spread(r2, xo * 576, delta, yy, lane)

    d1[...] = (jnp.dot(w2b[...], r2[...], preferred_element_type=F32) * sl1[...]).astype(BF)

    g2[0:1440, :] = lax.dot_general(q1[0:1440, :], d2[...], NT, preferred_element_type=F32)
    g2[1440:1472, :] = lax.dot_general(s1[288:320, :], d2[...], NT, preferred_element_type=F32)

    def tap_two(n):
        if n == 27:
            return sum(g2[1440:1472, p * C2 : (p + 1) * C2] for p in range(3))
        row = (n // 9) * 288 + (n % 9) * C1
        return sum(g2[row + p * 288 : row + p * 288 + C1, p * C2 : (p + 1) * C2] for p in range(3))

    def pack_b(i, rows):
        acc_b[0, i] = rows[0:16].astype(BF)
        acc_b[1, i] = rows[16:32].astype(BF)

    for i in range(14):
        pack_b(i, jnp.concatenate([tap_two(2 * i), tap_two(2 * i + 1)], axis=1))

    g1[...] = lax.dot_general(s1[0:320, :], d1[...], NT, preferred_element_type=F32)

    def tap_one(b):
        if b > 9:
            return jnp.zeros((16, C1), F32)
        if b == 9:
            return sum(g1[288:304, p * C1 : (p + 1) * C1] for p in range(5))
        return sum(g1[b * 32 + 4 * p : b * 32 + 4 * p + 16, p * C1 : (p + 1) * C1] for p in range(5))

    rows_one = [jnp.concatenate([tap_one(4 * g + i) for i in range(4)], axis=1) for g in range(3)]
    pack_b(14, jnp.concatenate(rows_one[0:2], axis=0))
    pack_b(15, jnp.concatenate([rows_one[2], jnp.zeros((16, ZS), F32)], axis=0))
    copy_b0 = pltpu.make_async_remote_copy(
        src_ref=acc_b.at[1 - c], dst_ref=rx_b0, send_sem=b_s.at[0], recv_sem=b_r.at[0], device_id=partner, device_id_type=MESH)
    copy_b0.start()
    leaving.append((True, copy_b0.wait_send))
    copy_b0.wait_recv()
    sum_b[...] = (acc_b[c].astype(F32) + rx_b0[...].astype(F32)).astype(BF)
    xy_scatter(sum_b, rx_b1, b_s.at[1], b_r.at[1])

    wait_bytes(rx_a1, a_r.at[1])
    z_a[zi] = (sum_a[rank].astype(F32) + total_of(rx_a1, 15)).astype(BF)
    z_gather(z_a, a_s.at[2], a_r.at[2])
    wait_bytes(rx_b1, b_r.at[1])
    z_b[zi] = (sum_b[rank].astype(F32) + total_of(rx_b1, 15)).astype(BF)
    z_gather(z_b, b_s.at[2], b_r.at[2])
    wait_bytes(z_a.at[pl.ds(0, 7)], a_r.at[2])
    half = gath_a.at[c]
    half[rank] = total_of(z_a, 8).astype(BF)
    xy_gather(half, a_s.at[3], a_r.at[3])
    wait_bytes(z_b.at[pl.ds(0, 7)], b_r.at[2])
    half_b = gath_b.at[c]
    half_b[rank] = total_of(z_b, 8).astype(BF)
    xy_gather(half_b, b_s.at[3], b_r.at[3])

    def write(i, src, dst):
        copy = pltpu.make_async_copy(src, dst, outs.at[i])
        copy.start()
        leaving.append((True, copy.wait))

    wait_bytes(half.at[pl.ds(0, 15)], a_r.at[3])
    copy_a4 = pltpu.make_async_remote_copy(
        src_ref=half, dst_ref=half, send_sem=a_s.at[4], recv_sem=a_r.at[4], device_id=partner, device_id_type=MESH)
    copy_a4.start()
    leaving.append((True, copy_a4.wait_send))
    write(1, half, out_a.at[c])

    wait_bytes(half_b.at[pl.ds(0, 15)], b_r.at[3])
    copy_b4 = pltpu.make_async_remote_copy(
        src_ref=half_b, dst_ref=half_b, send_sem=b_s.at[4], recv_sem=b_r.at[4], device_id=partner, device_id_type=MESH)
    copy_b4.start()
    leaving.append((True, copy_b4.wait_send))
    copy_a4.wait_recv()
    write(2, gath_a.at[1 - c], out_a.at[1 - c])
    copy_b4.wait_recv()
    write(0, gath_b, out_b)

    for cond, wait in leaving:
        if cond is True:
            wait()
        else:
            pl.when(cond)(wait)


def unpack(in_a, in_b, o1, ob1, o2, ob2, o3, ob3, gath_a, gath_b, v1, vb1, v2, vb2, v3, vb3, sems, ins):
    pairs = ((in_a.at[0], gath_a.at[0]), (in_a.at[1], gath_a.at[1]), (in_b, gath_b))
    loads = [pltpu.make_async_copy(src, dst, ins.at[i]) for i, (src, dst) in enumerate(pairs)]
    for load in loads:
        load.start()
    outs = (o3, o2, o1, ob1, ob2, ob3)
    copies = [pltpu.make_async_copy(v, o, sems.at[i]) for i, (v, o) in enumerate(zip((v3, v2, v1, vb1, vb2, vb3), outs))]
    loads[0].wait()
    loads[1].wait()
    for t in range(27):
        v3[t // 9, (t // 3) % 3, t % 3] = gath_a[t // 16, t % 16].astype(F32)
    copies[0].start()
    loads[2].wait()

    def rows_b(i):
        return jnp.concatenate([gath_b[0, i].astype(F32), gath_b[1, i].astype(F32)], axis=0)

    for t in range(27):
        i, s = t // 2, (t % 2) * 64
        v2[t // 9, (t // 3) % 3, t % 3] = rows_b(i)[:, s : s + 64]
    copies[1].start()
    fin = jnp.concatenate([rows_b(14), rows_b(15)], axis=0)
    for b in range(9):
        g, i = b // 4, b % 4
        for kx in range(3):
            v1[kx, b // 3, b % 3] = fin[g * 16 + kx * 4 : g * 16 + kx * 4 + 4, i * 32 : i * 32 + 32]
    copies[2].start()
    vb1[...] = fin[32:33, 32:64].reshape(C1)
    copies[3].start()
    vb2[...] = rows_b(13)[0:1, 64:128].reshape(C2)
    copies[4].start()
    vb3[...] = gath_a[1, 11].astype(F32)[0:1, :].reshape(C3)
    copies[5].start()
    for copy in copies:
        copy.wait()


def local(*args):
    V = pltpu.VMEM
    D = pltpu.SemaphoreType.DMA
    hbm = pl.BlockSpec(memory_space=pltpu.HBM)
    sums = pl.pallas_call(
        body,
        out_shape=(
            jax.ShapeDtypeStruct((2, 16, 64, ZS), BF),
            jax.ShapeDtypeStruct((2, 16, 16, ZS), BF),
        ),
        in_specs=[hbm] * 8,
        out_specs=(hbm,) * 2,
        scratch_shapes=[
            V((2, 16, 64, ZS), BF), V((2, 16, 16, ZS), BF), D((3,)),
            V((1, C0, 1, YS, ZS), BF), V((3, 3, 3, C0, C1), BF), V((C1,), F32), V((3, 3, 3, C1, C2), BF), V((C2,), F32),
            V((3, 3, 3, C2, C3), BF), V((C3,), F32), D((8,)),
            V((7, C0, YS, ZS), BF), V((1, C3, 1, YS, ZS), BF), V((C3 * YS, ZS), F32), V((256, ZS), F32),
            V((384, ZS), F32), V((160, 384), BF), V((192, 1536), BF), V((C3, 1792), BF), V((192, 1152), BF), V((160, 1792), BF),
            V((ZS, ZS), F32),
            V((384, CELLS), BF), V((1536, CELLS), BF), V((2048, CELLS), BF), V((1152, CELLS), BF), V((1792, CELLS), BF),
            V((192, CELLS), F32), V((C3, CELLS), BF), V((192, CELLS), BF), V((160, CELLS), BF), V((160, CELLS), F32), V((192, CELLS), F32),
            V((192, CELLS), F32),
            V((1024, ZS), BF), V((1024, ZS), F32), V((1024, ZS), BF), V((16, 64, ZS), BF), V((15, 64, ZS), BF), V((8, 64, ZS), BF),
            V((1472, 192), F32), V((2, 16, 16, ZS), BF), V((16, 16, ZS), BF), V((16, 16, ZS), BF), V((15, 16, ZS), BF), V((8, 16, ZS), BF),
            V((320, 160), F32),
            D((7,)), D((7,)), D((5,)), D((5,)), D((5,)), D((5,)), pltpu.SemaphoreType.REGULAR,
        ],
        compiler_params=pltpu.CompilerParams(collective_id=0, has_side_effects=True, vmem_limit_bytes=62 << 20),
        name="backward",
    )(*args)
    shapes = ((3, 3, 3, C0, C1), (C1,), (3, 3, 3, C1, C2), (C2,), (3, 3, 3, C2, C3), (C3,))
    return pl.pallas_call(
        unpack,
        out_shape=tuple(jax.ShapeDtypeStruct(s, F32) for s in shapes),
        in_specs=[hbm] * 2,
        out_specs=(hbm,) * 6,
        scratch_shapes=[V((2, 16, 64, ZS), BF), V((2, 16, 16, ZS), BF)]
        + [V(s, F32) for s in shapes]
        + [D((6,)), D((3,))],
        compiler_params=pltpu.CompilerParams(vmem_limit_bytes=62 << 20),
        name="widen",
    )(*sums)


def solution(mesh):
    placed = (
        P("sample", None, "space", None, None),
        P("sample", None, "space", None, None),
        P(), P(), P(), P(), P(), P(),
    )
    return jax.shard_map(local, mesh=mesh, in_specs=placed, out_specs=(P(),) * 6, check_vma=False)
```

```python
import math

import jax
import jax.numpy as jnp
from jax import lax
from jax.experimental import pallas as pl
from jax.experimental.pallas import tpu as pltpu
from jax.sharding import PartitionSpec as P

MESH = pl.DeviceIdType.MESH
BF = jnp.bfloat16
F32 = jnp.float32

C0, C1, C2, C3 = 4, 32, 64, 128
YS, ZS, NX = 8, 128, 16
CELLS = YS * ZS
SCALE = 1.0 / math.sqrt(16 * NX * YS * ZS)
NT = (((1,), (1,)), ((), ()))


def leaky(u):
    return 0.3 * u + 0.7 * (jnp.maximum(u, 0.0) + jnp.log(1.0 + jnp.exp(-jnp.abs(u))))


def slope(u):
    e = jnp.exp(-jnp.abs(u))
    r = 1.0 / (1.0 + e)
    return 0.3 + 0.7 * jnp.where(u >= 0.0, r, e * r)


def shifted(slab, lane):
    lo = jnp.where(lane == 0, 0.0, pltpu.roll(slab, 1, 1))
    hi = jnp.where(lane == ZS - 1, 0.0, pltpu.roll(slab, ZS - 1, 1))
    return lo.astype(BF), slab.astype(BF), hi.astype(BF)


def spread(ref, base, slab, ysrc, lane):
    width = slab.shape[0]
    parts = shifted(slab, lane)
    for ky in range(3):
        yo = ysrc + 1 - ky
        if 0 <= yo < YS:
            for kz in range(3):
                row = base + (ky * 3 + kz) * width
                ref[row : row + width, yo * ZS : (yo + 1) * ZS] = parts[kz]


def zero_edges(ref, base, width):
    for ky, yo in ((0, 0), (2, YS - 1)):
        row = base + ky * 3 * width
        ref[row : row + 3 * width, yo * ZS : (yo + 1) * ZS] = jnp.zeros((3 * width, ZS), BF)


def body(
    vol_h, cot, w1_h, b1_h, w2_h, b2_h, w3_h, b3_h,
    out_a, out_b, out_c,
    gath_a, gath_b, fin, outs,
    vol, w1, b1, w2, b2, w3, b3, ins,
    vols, cotv, cotf, volf, w1f, w1big, w2big, w3t, w3b, w2b, bcols,
    s1, q1, q2, r3, r2, pre1, pre2, pre3, d3, d2, d1, sl1, sl2, fl,
    acc_a, own_a, rx_a0, sum_a, rx_a1, z_a,
    g2, acc_b, rx_b0, sum_b, rx_b1, z_b,
    g1, acc_c, rx_c0, x_c, z_c,
    vs, vr, a_s, a_r, b_s, b_r, c_s, c_r, ready,
):
    me_s, me_p = lax.axis_index("sample"), lax.axis_index("space")
    zh, y, c = me_s // 8, (me_s // 2) % 4, me_s % 2
    x, zl = me_p // 4, me_p % 4
    rank = x * 4 + y
    zi = zh * 4 + zl
    partner = (me_s + 1 - 2 * c, me_p)

    def hops(d, n):
        return min(d, n - d)

    xy_peers = []
    for dx, dy in sorted([(i, j) for i in range(4) for j in range(4)], key=lambda o: -hops(o[0], 4) - hops(o[1], 4))[:15]:
        px, py = (x + dx) % 4, (y + dy) % 4
        xy_peers.append((px * 4 + py, (zh * 8 + py * 2 + c, px * 4 + zl)))
    z_peers = []
    for d in sorted(range(1, 8), key=lambda o: -hops(o, 8)):
        z = (zi + d) % 8
        z_peers.append(((z // 4) * 8 + y * 2 + c, x * 4 + z % 4))

    near = [(j, (me_p + j >= 0) & (me_p + j < NX)) for j in (1, -1, 2, -2, 3, -3)]

    leaving = []

    def drain():
        for cond, wait in leaving:
            if cond is True:
                wait()
            else:
                pl.when(cond)(wait)
        leaving.clear()

    loads = [
        pltpu.make_async_copy(src, dst, ins.at[i])
        for i, (src, dst) in enumerate(((vol_h, vol), (w1_h, w1), (b1_h, b1), (b2_h, b2), (b3_h, b3), (w2_h, w2), (w3_h, w3), (cot, cotv)))
    ]
    loads[0].start()

    x_line = [(me_s, (me_p + 4 * d) % 16) for d in (2, 1, 3)]
    y_line = [(zh * 8 + ((y + d) % 4) * 2 + c, me_p) for d in (2, 1, 3)]
    z_line = [(me_s, 4 * x + (zl + d) % 4) for d in (1, 2, 3)]
    barrier = pltpu.get_barrier_semaphore()
    count = jnp.int32(8)
    for j, ok in near:
        @pl.when(ok)
        def _():
            pl.semaphore_signal(barrier, 1, device_id=(me_s, me_p + j), device_id_type=MESH)
        count = count + ok.astype(jnp.int32)
    for dev in [((me_s + 8) % 16, me_p)] + x_line + y_line + [partner]:
        pl.semaphore_signal(barrier, 1, device_id=dev, device_id_type=MESH)

    lane = lax.broadcasted_iota(jnp.int32, (1, ZS), 1)
    loads[0].wait()
    pl.semaphore_wait(barrier, count)


    for j, ok in near:
        copy = pltpu.make_async_remote_copy(
            src_ref=vol.at[0, :, 0], dst_ref=vols.at[3 - j], send_sem=vs.at[3 + j], recv_sem=vr.at[3 - j],
            device_id=(me_s, me_p + j), device_id_type=MESH)
        pl.when(ok)(copy.start)
        leaving.append((ok, copy.wait_send))

    for load in loads[1:]:
        load.start()

    for dev in x_line + z_line:
        pl.semaphore_signal(ready, 1, device_id=dev, device_id_type=MESH)

    w1f[...] = jnp.zeros_like(w1f)
    for load in loads[1:5]:
        load.wait()
    for kx in range(3):
        for ky in range(3):
            for kz in range(3):
                row = (ky * 3 + kz) * 32 + kx * 4
                w1f[row : row + 4, 0:C1] = w1[kx, ky, kz].astype(F32)
    t1 = w1f[...].T[0:C1]
    for xo in range(5):
        w1big[xo * C1 : (xo + 1) * C1, :] = (pltpu.roll(t1, 4 * xo, 1) if xo else t1).astype(BF)
    bcols[...] = jnp.zeros_like(bcols)
    bcols[:, 0:C1] = jnp.broadcast_to(b1[...].reshape(1, C1), (ZS, C1))
    bcols[:, C2 : 2 * C2] = jnp.broadcast_to(b2[...].reshape(1, C2), (ZS, C2))
    bt = bcols[...].T
    bcols[...] = bt
    b3col = jnp.broadcast_to(b3[...].reshape(1, C3), (ZS, C3)).T
    s1[288:320, :] = jnp.ones((32, CELLS), BF)
    s1[320:384, :] = jnp.zeros((64, CELLS), BF)
    zero_edges(s1, 0, 32)
    for xo in range(5):
        zero_edges(q1, xo * 288, C1)
    q1[1440:1472, :] = jnp.ones((32, CELLS), BF)
    q1[1472:1536, :] = jnp.zeros((64, CELLS), BF)
    for xo in range(3):
        zero_edges(q2, xo * 576, C2)
    q2[1728:1744, :] = jnp.ones((16, CELLS), BF)
    q2[1744:2048, :] = jnp.zeros((304, CELLS), BF)
    zero_edges(r3, 0, C3)
    for xo in range(3):
        zero_edges(r2, xo * 576, C2)
    r2[1728:1792, :] = jnp.zeros((64, CELLS), BF)
    volf[224:256, :] = jnp.zeros((32, ZS), F32)

    for load in loads[5:]:
        load.wait()
    vols[3] = vol[0, :, 0]
    cotf[...] = cotv[...].reshape(C3, YS, ZS).astype(F32).reshape(C3 * YS, ZS)
    t2 = jnp.concatenate([w2[...].reshape(864, C2).astype(F32), jnp.zeros((32, C2), F32)], axis=0)
    t2 = jnp.concatenate([t2, jnp.zeros((896, C2), F32)], axis=1).T[0:C2]
    t2 = jnp.concatenate([t2, jnp.zeros((C2, 640), F32)], axis=1)
    for xo in range(3):
        w2big[xo * C2 : (xo + 1) * C2, :] = (pltpu.roll(t2, 288 * xo, 1) if xo else t2).astype(BF)
    w3t[:, 0:1728] = w3[...].reshape(1728, C3).astype(F32).T.astype(BF)
    w3t[:, 1728:1792] = jnp.zeros((C3, 64), BF)
    for kx in range(3):
        for t in range(9):
            ky, kz = 2 - t // 3, 2 - t % 3
            w3b[kx * C2 : (kx + 1) * C2, t * C3 : (t + 1) * C3] = w3[kx, ky, kz]
    def back_tap(xo, n):
        plane, t = n // 9, n % 9
        kx = xo - plane
        if n >= 27 or not 0 <= kx < 3:
            return jnp.zeros((C1, C2), F32)
        return w2[kx, 2 - t // 3, 2 - t % 3].astype(F32)

    for xo in range(5):
        for n in range(0, 28, 2):
            both = jnp.concatenate([back_tap(xo, n), back_tap(xo, n + 1)], axis=1)
            w2b[xo * C1 : (xo + 1) * C1, n * C2 : (n + 2) * C2] = both.astype(BF)

    pl.semaphore_wait(ready, 6)

    for j, ok in near:
        @pl.when(ok)
        def _():
            pltpu.make_async_copy(vols.at[3 + j], vols.at[3 + j], vr.at[3 + j]).wait()

        @pl.when(jnp.logical_not(ok))
        def _():
            vols[3 + j] = jnp.zeros((C0, YS, ZS), BF)
    volf[0:224, :] = vols[...].astype(F32).reshape(224, ZS)
    for yy in range(YS):
        spread(s1, 0, volf[pl.ds(yy, 32, stride=YS), :], yy, lane)

    def alive(plane):
        return jnp.where((plane >= 0) & (plane < NX), 1.0, 0.0).astype(F32)

    def slopes(sl, pre, bias, planes, width):
        for xo in range(planes):
            rows = slice(xo * width, (xo + 1) * width)
            live = alive(me_p + xo - planes // 2)
            for yy in range(YS):
                cut = slice(yy * ZS, (yy + 1) * ZS)
                sl[rows, cut] = slope(pre[rows, cut] + bias) * live

    pre1[...] = jnp.dot(w1big[...], s1[...], preferred_element_type=F32)
    for xo in range(5):
        plane = me_p + xo - 2
        live = alive(plane)
        for yy in range(YS):
            u = pre1[xo * C1 : (xo + 1) * C1, yy * ZS : (yy + 1) * ZS] + bcols[0:C1, :]
            a = leaky(u)
            spread(q1, xo * 288, a * live, yy, lane)

    pre2[...] = jnp.dot(w2big[...], q1[...], preferred_element_type=F32)
    for xo in range(3):
        plane = me_p + xo - 1
        live = alive(plane)
        for yy in range(YS):
            u = pre2[xo * C2 : (xo + 1) * C2, yy * ZS : (yy + 1) * ZS] + bcols[C2 : 2 * C2, :]
            a = leaky(u)
            spread(q2, xo * 576, a * live, yy, lane)

    pre3[...] = jnp.dot(w3t[...], q2[0:1792, :], preferred_element_type=F32)
    for yy in range(YS):
        u = pre3[:, yy * ZS : (yy + 1) * ZS] + b3col
        delta = cotf[pl.ds(yy, C3, stride=YS), :] * SCALE * slope(u)
        d3[:, yy * ZS : (yy + 1) * ZS] = delta.astype(BF)
        spread(r3, 0, delta, yy, lane)

    def xy_scatter(total, rx, send_sem, recv_sem):
        for n, (r, dev) in enumerate(xy_peers):
            pltpu.make_async_remote_copy(
                src_ref=total.at[r], dst_ref=rx.at[n], send_sem=send_sem, recv_sem=recv_sem,
                device_id=dev, device_id_type=MESH).start()
        leaving.append((True, lambda: wait_bytes(rx, send_sem)))

    def xy_gather(buf, send_sem, recv_sem):
        for _, dev in xy_peers:
            pltpu.make_async_remote_copy(
                src_ref=buf.at[rank], dst_ref=buf.at[rank], send_sem=send_sem, recv_sem=recv_sem,
                device_id=dev, device_id_type=MESH).start()
        leaving.append((True, lambda: wait_bytes(buf.at[pl.ds(0, 15)], send_sem)))

    def z_gather(buf, send_sem, recv_sem):
        for dev in z_peers:
            pltpu.make_async_remote_copy(
                src_ref=buf.at[zi], dst_ref=buf.at[zi], send_sem=send_sem, recv_sem=recv_sem,
                device_id=dev, device_id_type=MESH).start()
        leaving.append((True, lambda: wait_bytes(buf.at[pl.ds(0, 7)], send_sem)))

    def wait_bytes(ref, sem):
        pltpu.make_async_copy(ref, ref, sem).wait()

    def total_of(ref, n):
        t = ref[0].astype(F32)
        for i in range(1, n):
            t = t + ref[i].astype(F32)
        return t

    other = pl.multiple_of((1 - c) * 1024, 1024)
    mine = pl.multiple_of(c * 1024, 1024)
    acc_a[...] = lax.dot_general(q2[pl.ds(other, 1024), :], d3[...], NT, preferred_element_type=F32).astype(BF)
    copy_a0 = pltpu.make_async_remote_copy(
        src_ref=acc_a, dst_ref=rx_a0, send_sem=a_s.at[0], recv_sem=a_r.at[0],
        device_id=partner, device_id_type=MESH)
    copy_a0.start()
    leaving.append((True, copy_a0.wait_send))

    own_a[...] = lax.dot_general(q2[pl.ds(mine, 1024), :], d3[...], NT, preferred_element_type=F32)

    slopes(sl2, pre2, bcols[C2 : 2 * C2, :], 3, C2)

    fl[...] = jnp.dot(w3b[...], r3[...], preferred_element_type=F32)

    copy_a0.wait_recv()
    sum_a[...] = (own_a[...] + rx_a0[...].astype(F32)).astype(BF).reshape(16, 64, ZS)
    xy_scatter(sum_a, rx_a1, a_s.at[1], a_r.at[1])

    for xo in range(3):
        rows = slice(xo * C2, (xo + 1) * C2)
        for yy in range(YS):
            cut = slice(yy * ZS, (yy + 1) * ZS)
            delta = fl[rows, cut] * sl2[rows, cut]
            d2[rows, cut] = delta.astype(BF)
            spread(r2, xo * 576, delta, yy, lane)

    g2[...] = lax.dot_general(q1[0:1472, :], d2[...], NT, preferred_element_type=F32)

    def tap_two(n):
        if n == 27:
            return sum(g2[1440:1472, p * C2 : (p + 1) * C2] for p in range(3))
        row = (n // 9) * 288 + (n % 9) * C1
        return sum(g2[row + p * 288 : row + p * 288 + C1, p * C2 : (p + 1) * C2] for p in range(3))

    def pack_b(i, rows):
        acc_b[0, i] = rows[0:16].astype(BF)
        acc_b[1, i] = rows[16:32].astype(BF)

    for i in (14, 15):
        pack_b(i, jnp.zeros((32, ZS), F32))
    for i in range(14):
        pack_b(i, jnp.concatenate([tap_two(2 * i), tap_two(2 * i + 1)], axis=1))

    copy_b0 = pltpu.make_async_remote_copy(
        src_ref=acc_b.at[1 - c], dst_ref=rx_b0, send_sem=b_s.at[0], recv_sem=b_r.at[0], device_id=partner, device_id_type=MESH)
    copy_b0.start()
    leaving.append((True, copy_b0.wait_send))

    slopes(sl1, pre1, bcols[0:C1, :], 5, C1)

    d1[...] = (jnp.dot(w2b[...], r2[...], preferred_element_type=F32) * sl1[...]).astype(BF)

    copy_b0.wait_recv()
    sum_b[...] = (acc_b[c].astype(F32) + rx_b0[...].astype(F32)).astype(BF)
    xy_scatter(sum_b, rx_b1, b_s.at[1], b_r.at[1])

    g1[...] = lax.dot_general(s1[0:320, :], d1[...], NT, preferred_element_type=F32)

    def tap_one(b):
        if b > 9:
            return jnp.zeros((16, C1), F32)
        if b == 9:
            return sum(g1[288:304, p * C1 : (p + 1) * C1] for p in range(5))
        return sum(g1[b * 32 + 4 * p : b * 32 + 4 * p + 16, p * C1 : (p + 1) * C1] for p in range(5))

    for g in range(3):
        acc_c[g * 16 : (g + 1) * 16, :] = jnp.concatenate([tap_one(4 * g + i) for i in range(4)], axis=1).astype(BF)
    copy_c0 = pltpu.make_async_remote_copy(
        src_ref=acc_c, dst_ref=rx_c0, send_sem=c_s.at[0], recv_sem=c_r.at[0], device_id=partner, device_id_type=MESH)
    copy_c0.start()
    leaving.append((True, copy_c0.wait_send))
    copy_c0.wait_recv()
    x_c[rank] = (acc_c[...].astype(F32) + rx_c0[...].astype(F32)).astype(BF)
    xy_gather(x_c, c_s.at[1], c_r.at[1])

    wait_bytes(rx_a1, a_r.at[1])
    z_a[zi] = (sum_a[rank].astype(F32) + total_of(rx_a1, 15)).astype(BF)
    z_gather(z_a, a_s.at[2], a_r.at[2])
    wait_bytes(rx_b1, b_r.at[1])
    z_b[zi] = (sum_b[rank].astype(F32) + total_of(rx_b1, 15)).astype(BF)
    z_gather(z_b, b_s.at[2], b_r.at[2])
    wait_bytes(z_a.at[pl.ds(0, 7)], a_r.at[2])
    half = gath_a.at[c]
    half[rank] = total_of(z_a, 8).astype(BF)
    xy_gather(half, a_s.at[3], a_r.at[3])
    wait_bytes(x_c.at[pl.ds(0, 15)], c_r.at[1])
    z_c[zi] = total_of(x_c, 16).astype(BF)
    z_gather(z_c, c_s.at[2], c_r.at[2])
    wait_bytes(z_b.at[pl.ds(0, 7)], b_r.at[2])
    half_b = gath_b.at[c]
    half_b[rank] = total_of(z_b, 8).astype(BF)
    xy_gather(half_b, b_s.at[3], b_r.at[3])

    def write(i, src, dst):
        copy = pltpu.make_async_copy(src, dst, outs.at[i])
        copy.start()
        leaving.append((True, copy.wait))

    drain()

    wait_bytes(z_c.at[pl.ds(0, 7)], c_r.at[2])
    fin[...] = total_of(z_c, 8)
    write(0, fin, out_c)

    def to_partner(i, src, dst, send_sem, recv_sem):
        copy = pltpu.make_async_remote_copy(
            src_ref=src, dst_ref=dst, send_sem=send_sem, recv_sem=recv_sem, device_id=partner, device_id_type=MESH)
        copy.start()
        write(i, src, dst)
        leaving.append((True, copy.wait))

    wait_bytes(half.at[pl.ds(0, 15)], a_r.at[3])
    to_partner(1, half, out_a.at[c], a_s.at[4], a_r.at[4])
    wait_bytes(half_b.at[pl.ds(0, 15)], b_r.at[3])
    to_partner(2, half_b, out_b.at[c], b_s.at[4], b_r.at[4])

    drain()


def unpack(in_a, in_b, in_c, o1, ob1, o2, ob2, o3, ob3, gath_a, gath_b, fin, v1, vb1, v2, vb2, v3, vb3, sems, ins):
    pairs = ((in_a.at[0], gath_a.at[0]), (in_a.at[1], gath_a.at[1]), (in_b, gath_b), (in_c, fin))
    loads = [pltpu.make_async_copy(src, dst, ins.at[i]) for i, (src, dst) in enumerate(pairs)]
    for load in loads:
        load.start()
    started = []

    def write(src, dst):
        copy = pltpu.make_async_copy(src, dst, sems.at[len(started)])
        copy.start()
        started.append(copy)

    def rows_b(i):
        return jnp.concatenate([gath_b[0, i].astype(F32), gath_b[1, i].astype(F32)], axis=0)

    for kx in range(3):
        if kx == 0:
            loads[0].wait()
        for t in range(9 * kx, 9 * kx + 9):
            if t == 16:
                loads[1].wait()
            v3[t // 9, (t // 3) % 3, t % 3] = gath_a[t // 16, t % 16].astype(F32)
        write(v3.at[kx], o3.at[kx])
    vb3[...] = gath_a[1, 11].astype(F32)[0:1, :].reshape(C3)
    write(vb3, ob3)
    loads[2].wait()
    for t in range(27):
        i, s = t // 2, (t % 2) * 64
        v2[t // 9, (t // 3) % 3, t % 3] = rows_b(i)[:, s : s + 64]
    write(v2, o2)
    vb2[...] = rows_b(13)[0:1, 64:128].reshape(C2)
    write(vb2, ob2)
    loads[3].wait()
    for b in range(9):
        g, i = b // 4, b % 4
        for kx in range(3):
            v1[kx, b // 3, b % 3] = fin[g * 16 + kx * 4 : g * 16 + kx * 4 + 4, i * 32 : i * 32 + 32]
    write(v1, o1)
    vb1[...] = fin[32:33, 32:64].reshape(C1)
    write(vb1, ob1)
    for copy in started:
        copy.wait()


def local(*args):
    V = pltpu.VMEM
    D = pltpu.SemaphoreType.DMA
    hbm = pl.BlockSpec(memory_space=pltpu.HBM)
    sums = pl.pallas_call(
        body,
        out_shape=(
            jax.ShapeDtypeStruct((2, 16, 64, ZS), BF),
            jax.ShapeDtypeStruct((2, 16, 16, ZS), BF),
            jax.ShapeDtypeStruct((48, ZS), F32),
        ),
        in_specs=[hbm] * 8,
        out_specs=(hbm,) * 3,
        scratch_shapes=[
            V((2, 16, 64, ZS), BF), V((2, 16, 16, ZS), BF), V((48, ZS), F32), D((3,)),
            V((1, C0, 1, YS, ZS), BF), V((3, 3, 3, C0, C1), BF), V((C1,), F32), V((3, 3, 3, C1, C2), BF), V((C2,), F32),
            V((3, 3, 3, C2, C3), BF), V((C3,), F32), D((8,)),
            V((7, C0, YS, ZS), BF), V((1, C3, 1, YS, ZS), BF), V((C3 * YS, ZS), F32), V((256, ZS), F32),
            V((384, ZS), F32), V((160, 384), BF), V((192, 1536), BF), V((C3, 1792), BF), V((192, 1152), BF), V((160, 1792), BF),
            V((ZS, ZS), F32),
            V((384, CELLS), BF), V((1536, CELLS), BF), V((2048, CELLS), BF), V((1152, CELLS), BF), V((1792, CELLS), BF),
            V((160, CELLS), F32), V((192, CELLS), F32), V((C3, CELLS), F32), V((C3, CELLS), BF), V((192, CELLS), BF), V((160, CELLS), BF), V((160, CELLS), F32), V((192, CELLS), F32),
            V((192, CELLS), F32),
            V((1024, ZS), BF), V((1024, ZS), F32), V((1024, ZS), BF), V((16, 64, ZS), BF), V((15, 64, ZS), BF), V((8, 64, ZS), BF),
            V((1472, 192), F32), V((2, 16, 16, ZS), BF), V((16, 16, ZS), BF), V((16, 16, ZS), BF), V((15, 16, ZS), BF), V((8, 16, ZS), BF),
            V((320, 160), F32), V((48, ZS), BF), V((48, ZS), BF), V((16, 48, ZS), BF), V((8, 48, ZS), BF),
            D((7,)), D((7,)), D((5,)), D((5,)), D((5,)), D((5,)), D((3,)), D((3,)), pltpu.SemaphoreType.REGULAR,
        ],
        compiler_params=pltpu.CompilerParams(collective_id=0, has_side_effects=True, vmem_limit_bytes=62 << 20),
        name="backward",
    )(*args)
    shapes = ((3, 3, 3, C0, C1), (C1,), (3, 3, 3, C1, C2), (C2,), (3, 3, 3, C2, C3), (C3,))
    return pl.pallas_call(
        unpack,
        out_shape=tuple(jax.ShapeDtypeStruct(s, F32) for s in shapes),
        in_specs=[hbm] * 3,
        out_specs=(hbm,) * 6,
        scratch_shapes=[V((2, 16, 64, ZS), BF), V((2, 16, 16, ZS), BF), V((48, ZS), F32)]
        + [V(s, F32) for s in shapes]
        + [D((8,)), D((4,))],
        compiler_params=pltpu.CompilerParams(vmem_limit_bytes=62 << 20),
        name="widen",
    )(*sums)


def solution(mesh):
    placed = (
        P("sample", None, "space", None, None),
        P("sample", None, "space", None, None),
        P(), P(), P(), P(), P(), P(),
    )
    return jax.shard_map(local, mesh=mesh, in_specs=placed, out_specs=(P(),) * 6, check_vma=False)
```

```python
import math

import jax
import jax.numpy as jnp
from jax import lax
from jax.experimental import pallas as pl
from jax.experimental.pallas import tpu as pltpu
from jax.sharding import PartitionSpec as P

MESH = pl.DeviceIdType.MESH
BF = jnp.bfloat16
F32 = jnp.float32

C0, C1, C2, C3 = 4, 32, 64, 128
YS, ZS, NX = 8, 128, 16
CELLS = YS * ZS
SCALE = 1.0 / math.sqrt(16 * NX * YS * ZS)
NT = (((1,), (1,)), ((), ()))


def leaky(u):
    return 0.3 * u + 0.7 * (jnp.maximum(u, 0.0) + jnp.log(1.0 + jnp.exp(-jnp.abs(u))))


def slope(u):
    e = jnp.exp(-jnp.abs(u))
    r = 1.0 / (1.0 + e)
    return 0.3 + 0.7 * jnp.where(u >= 0.0, r, e * r)


def shifted(slab, lane):
    lo = jnp.where(lane == 0, 0.0, pltpu.roll(slab, 1, 1))
    hi = jnp.where(lane == ZS - 1, 0.0, pltpu.roll(slab, ZS - 1, 1))
    return lo.astype(BF), slab.astype(BF), hi.astype(BF)


def spread(ref, base, slab, ysrc, lane):
    width = slab.shape[0]
    parts = shifted(slab, lane)
    for ky in range(3):
        yo = ysrc + 1 - ky
        if 0 <= yo < YS:
            for kz in range(3):
                row = base + (ky * 3 + kz) * width
                ref[row : row + width, yo * ZS : (yo + 1) * ZS] = parts[kz]


def zero_edges(ref, base, width):
    for ky, yo in ((0, 0), (2, YS - 1)):
        row = base + ky * 3 * width
        ref[row : row + 3 * width, yo * ZS : (yo + 1) * ZS] = jnp.zeros((3 * width, ZS), BF)


def body(
    vol_h, cot, w1_h, b1_h, w2_h, b2_h, w3_h, b3_h,
    out_a, out_b, out_c,
    gath_a, gath_b, fin, outs,
    vol, w1, b1, w2, b2, w3, b3, ins,
    vols, cotv, cotf, volf, w1f, w1big, w2big, w3t, w3b, w2b, bcols,
    s1, q1, q2, r3, r2, pre1, pre2, pre3, d3, d2, d1, sl1, sl2, fl,
    acc_a, own_a, rx_a0, sum_a, rx_a1, z_a,
    g2, acc_b, rx_b0, sum_b, rx_b1, z_b,
    g1, acc_c, rx_c0, x_c, z_c,
    vs, vr, a_s, a_r, b_s, b_r, c_s, c_r, ready,
):
    me_s, me_p = lax.axis_index("sample"), lax.axis_index("space")
    zh, y, c = me_s // 8, (me_s // 2) % 4, me_s % 2
    x, zl = me_p // 4, me_p % 4
    rank = x * 4 + y
    zi = zh * 4 + zl
    partner = (me_s + 1 - 2 * c, me_p)

    def hops(d, n):
        return min(d, n - d)

    xy_peers = []
    for dx, dy in sorted([(i, j) for i in range(4) for j in range(4)], key=lambda o: -hops(o[0], 4) - hops(o[1], 4))[:15]:
        px, py = (x + dx) % 4, (y + dy) % 4
        xy_peers.append((px * 4 + py, (zh * 8 + py * 2 + c, px * 4 + zl)))
    z_peers = []
    for d in sorted(range(1, 8), key=lambda o: -hops(o, 8)):
        z = (zi + d) % 8
        z_peers.append(((z // 4) * 8 + y * 2 + c, x * 4 + z % 4))

    near = [(j, (me_p + j >= 0) & (me_p + j < NX)) for j in (1, -1, 2, -2, 3, -3)]

    leaving = []

    def drain():
        for cond, wait in leaving:
            if cond is True:
                wait()
            else:
                pl.when(cond)(wait)
        leaving.clear()

    loads = [
        pltpu.make_async_copy(src, dst, ins.at[i])
        for i, (src, dst) in enumerate(((vol_h, vol), (w1_h, w1), (b1_h, b1), (b2_h, b2), (b3_h, b3), (w2_h, w2), (w3_h, w3), (cot, cotv)))
    ]
    loads[0].start()

    x_line = [(me_s, (me_p + 4 * d) % 16) for d in (2, 1, 3)]
    y_line = [(zh * 8 + ((y + d) % 4) * 2 + c, me_p) for d in (2, 1, 3)]
    z_line = [(me_s, 4 * x + (zl + d) % 4) for d in (1, 2, 3)]
    barrier = pltpu.get_barrier_semaphore()
    count = jnp.int32(8)
    for j, ok in near:
        @pl.when(ok)
        def _():
            pl.semaphore_signal(barrier, 1, device_id=(me_s, me_p + j), device_id_type=MESH)
        count = count + ok.astype(jnp.int32)
    for dev in [((me_s + 8) % 16, me_p)] + x_line + y_line + [partner]:
        pl.semaphore_signal(barrier, 1, device_id=dev, device_id_type=MESH)

    lane = lax.broadcasted_iota(jnp.int32, (1, ZS), 1)
    loads[0].wait()
    pl.semaphore_wait(barrier, count)


    for j, ok in near:
        copy = pltpu.make_async_remote_copy(
            src_ref=vol.at[0, :, 0], dst_ref=vols.at[3 - j], send_sem=vs.at[3 + j], recv_sem=vr.at[3 - j],
            device_id=(me_s, me_p + j), device_id_type=MESH)
        pl.when(ok)(copy.start)
        leaving.append((ok, copy.wait_send))

    for load in loads[1:]:
        load.start()

    for dev in x_line + z_line:
        pl.semaphore_signal(ready, 1, device_id=dev, device_id_type=MESH)

    w1f[...] = jnp.zeros_like(w1f)
    for load in loads[1:5]:
        load.wait()
    for kx in range(3):
        for ky in range(3):
            for kz in range(3):
                row = (ky * 3 + kz) * 32 + kx * 4
                w1f[row : row + 4, 0:C1] = w1[kx, ky, kz].astype(F32)
    t1 = w1f[...].T[0:C1]
    for xo in range(5):
        w1big[xo * C1 : (xo + 1) * C1, :] = (pltpu.roll(t1, 4 * xo, 1) if xo else t1).astype(BF)
    bcols[...] = jnp.zeros_like(bcols)
    bcols[:, 0:C1] = jnp.broadcast_to(b1[...].reshape(1, C1), (ZS, C1))
    bcols[:, C2 : 2 * C2] = jnp.broadcast_to(b2[...].reshape(1, C2), (ZS, C2))
    bt = bcols[...].T
    bcols[...] = bt
    b3col = jnp.broadcast_to(b3[...].reshape(1, C3), (ZS, C3)).T
    s1[288:320, :] = jnp.ones((32, CELLS), BF)
    s1[320:384, :] = jnp.zeros((64, CELLS), BF)
    zero_edges(s1, 0, 32)
    for xo in range(5):
        zero_edges(q1, xo * 288, C1)
    q1[1440:1472, :] = jnp.ones((32, CELLS), BF)
    q1[1472:1536, :] = jnp.zeros((64, CELLS), BF)
    for xo in range(3):
        zero_edges(q2, xo * 576, C2)
    q2[1728:1744, :] = jnp.ones((16, CELLS), BF)
    q2[1744:2048, :] = jnp.zeros((304, CELLS), BF)
    zero_edges(r3, 0, C3)
    for xo in range(3):
        zero_edges(r2, xo * 576, C2)
    r2[1728:1792, :] = jnp.zeros((64, CELLS), BF)
    volf[224:256, :] = jnp.zeros((32, ZS), F32)

    for load in loads[5:]:
        load.wait()
    vols[3] = vol[0, :, 0]
    cotf[...] = cotv[...].reshape(C3, YS, ZS).astype(F32).reshape(C3 * YS, ZS)
    t2 = jnp.concatenate([w2[...].reshape(864, C2).astype(F32), jnp.zeros((32, C2), F32)], axis=0)
    t2 = jnp.concatenate([t2, jnp.zeros((896, C2), F32)], axis=1).T[0:C2]
    t2 = jnp.concatenate([t2, jnp.zeros((C2, 640), F32)], axis=1)
    for xo in range(3):
        w2big[xo * C2 : (xo + 1) * C2, :] = (pltpu.roll(t2, 288 * xo, 1) if xo else t2).astype(BF)
    w3t[:, 0:1728] = w3[...].reshape(1728, C3).astype(F32).T.astype(BF)
    w3t[:, 1728:1792] = jnp.zeros((C3, 64), BF)
    for kx in range(3):
        for t in range(9):
            ky, kz = 2 - t // 3, 2 - t % 3
            w3b[kx * C2 : (kx + 1) * C2, t * C3 : (t + 1) * C3] = w3[kx, ky, kz]
    def back_tap(xo, n):
        plane, t = n // 9, n % 9
        kx = xo - plane
        if n >= 27 or not 0 <= kx < 3:
            return jnp.zeros((C1, C2), F32)
        return w2[kx, 2 - t // 3, 2 - t % 3].astype(F32)

    for xo in range(5):
        for n in range(0, 28, 2):
            both = jnp.concatenate([back_tap(xo, n), back_tap(xo, n + 1)], axis=1)
            w2b[xo * C1 : (xo + 1) * C1, n * C2 : (n + 2) * C2] = both.astype(BF)

    pl.semaphore_wait(ready, 6)

    for j, ok in near:
        @pl.when(ok)
        def _():
            pltpu.make_async_copy(vols.at[3 + j], vols.at[3 + j], vr.at[3 + j]).wait()

        @pl.when(jnp.logical_not(ok))
        def _():
            vols[3 + j] = jnp.zeros((C0, YS, ZS), BF)
    volf[0:224, :] = vols[...].astype(F32).reshape(224, ZS)
    for yy in range(YS):
        spread(s1, 0, volf[pl.ds(yy, 32, stride=YS), :], yy, lane)

    def alive(plane):
        return jnp.where((plane >= 0) & (plane < NX), 1.0, 0.0).astype(F32)

    def slopes(sl, pre, bias, planes, width):
        for xo in range(planes):
            rows = slice(xo * width, (xo + 1) * width)
            live = alive(me_p + xo - planes // 2)
            for yy in range(YS):
                cut = slice(yy * ZS, (yy + 1) * ZS)
                sl[rows, cut] = slope(pre[rows, cut] + bias) * live

    pre1[...] = jnp.dot(w1big[...], s1[...], preferred_element_type=F32)
    for xo in range(5):
        plane = me_p + xo - 2
        live = alive(plane)
        for yy in range(YS):
            u = pre1[xo * C1 : (xo + 1) * C1, yy * ZS : (yy + 1) * ZS] + bcols[0:C1, :]
            a = leaky(u)
            spread(q1, xo * 288, a * live, yy, lane)

    pre2[...] = jnp.dot(w2big[...], q1[...], preferred_element_type=F32)
    for xo in range(3):
        plane = me_p + xo - 1
        live = alive(plane)
        for yy in range(YS):
            u = pre2[xo * C2 : (xo + 1) * C2, yy * ZS : (yy + 1) * ZS] + bcols[C2 : 2 * C2, :]
            a = leaky(u)
            spread(q2, xo * 576, a * live, yy, lane)

    pre3[...] = jnp.dot(w3t[...], q2[0:1792, :], preferred_element_type=F32)
    for yy in range(YS):
        u = pre3[:, yy * ZS : (yy + 1) * ZS] + b3col
        delta = cotf[pl.ds(yy, C3, stride=YS), :] * SCALE * slope(u)
        d3[:, yy * ZS : (yy + 1) * ZS] = delta.astype(BF)
        spread(r3, 0, delta, yy, lane)

    def xy_scatter(total, rx, send_sem, recv_sem):
        for n, (r, dev) in enumerate(xy_peers):
            pltpu.make_async_remote_copy(
                src_ref=total.at[r], dst_ref=rx.at[n], send_sem=send_sem, recv_sem=recv_sem,
                device_id=dev, device_id_type=MESH).start()
        leaving.append((True, lambda: wait_bytes(rx, send_sem)))

    def xy_gather(buf, send_sem, recv_sem):
        for _, dev in xy_peers:
            pltpu.make_async_remote_copy(
                src_ref=buf.at[rank], dst_ref=buf.at[rank], send_sem=send_sem, recv_sem=recv_sem,
                device_id=dev, device_id_type=MESH).start()
        leaving.append((True, lambda: wait_bytes(buf.at[pl.ds(0, 15)], send_sem)))

    def z_gather(buf, send_sem, recv_sem):
        for dev in z_peers:
            pltpu.make_async_remote_copy(
                src_ref=buf.at[zi], dst_ref=buf.at[zi], send_sem=send_sem, recv_sem=recv_sem,
                device_id=dev, device_id_type=MESH).start()
        leaving.append((True, lambda: wait_bytes(buf.at[pl.ds(0, 7)], send_sem)))

    def wait_bytes(ref, sem):
        pltpu.make_async_copy(ref, ref, sem).wait()

    def total_of(ref, n):
        t = ref[0].astype(F32)
        for i in range(1, n):
            t = t + ref[i].astype(F32)
        return t

    other = pl.multiple_of((1 - c) * 896, 896)
    mine = pl.multiple_of(c * 896, 896)
    acc_a[...] = lax.dot_general(q2[pl.ds(other, 896), :], d3[...], NT, preferred_element_type=F32).astype(BF)
    copy_a0 = pltpu.make_async_remote_copy(
        src_ref=acc_a, dst_ref=rx_a0, send_sem=a_s.at[0], recv_sem=a_r.at[0],
        device_id=partner, device_id_type=MESH)
    copy_a0.start()
    leaving.append((True, copy_a0.wait_send))

    own_a[...] = lax.dot_general(q2[pl.ds(mine, 896), :], d3[...], NT, preferred_element_type=F32)

    slopes(sl2, pre2, bcols[C2 : 2 * C2, :], 3, C2)

    fl[...] = jnp.dot(w3b[...], r3[...], preferred_element_type=F32)

    copy_a0.wait_recv()
    sum_a[...] = (own_a[...] + rx_a0[...].astype(F32)).astype(BF).reshape(14, 64, ZS)
    for n, (r, dev) in enumerate(xy_peers):
        chunk = r - (r // 14) * (r - 13)
        copy = pltpu.make_async_remote_copy(
            src_ref=sum_a.at[chunk], dst_ref=rx_a1.at[n], send_sem=a_s.at[1], recv_sem=a_r.at[1],
            device_id=dev, device_id_type=MESH)
        pl.when(r < 14)(copy.start)
    owner, idle = rank < 14, rank >= 14
    leaving.append((owner, lambda: wait_bytes(rx_a1.at[pl.ds(0, 13)], a_s.at[1])))
    leaving.append((idle, lambda: wait_bytes(rx_a1.at[pl.ds(0, 14)], a_s.at[1])))

    for xo in range(3):
        rows = slice(xo * C2, (xo + 1) * C2)
        for yy in range(YS):
            cut = slice(yy * ZS, (yy + 1) * ZS)
            delta = fl[rows, cut] * sl2[rows, cut]
            d2[rows, cut] = delta.astype(BF)
            spread(r2, xo * 576, delta, yy, lane)

    g2[...] = lax.dot_general(q1[0:1472, :], d2[...], NT, preferred_element_type=F32)

    def tap_two(n):
        if n == 27:
            return sum(g2[1440:1472, p * C2 : (p + 1) * C2] for p in range(3))
        row = (n // 9) * 288 + (n % 9) * C1
        return sum(g2[row + p * 288 : row + p * 288 + C1, p * C2 : (p + 1) * C2] for p in range(3))

    def pack_b(i, rows):
        acc_b[0, i] = rows[0:16].astype(BF)
        acc_b[1, i] = rows[16:32].astype(BF)

    for i in (14, 15):
        pack_b(i, jnp.zeros((32, ZS), F32))
    for i in range(14):
        pack_b(i, jnp.concatenate([tap_two(2 * i), tap_two(2 * i + 1)], axis=1))

    copy_b0 = pltpu.make_async_remote_copy(
        src_ref=acc_b.at[1 - c], dst_ref=rx_b0, send_sem=b_s.at[0], recv_sem=b_r.at[0], device_id=partner, device_id_type=MESH)
    copy_b0.start()
    leaving.append((True, copy_b0.wait_send))

    slopes(sl1, pre1, bcols[0:C1, :], 5, C1)

    d1[...] = (jnp.dot(w2b[...], r2[...], preferred_element_type=F32) * sl1[...]).astype(BF)

    copy_b0.wait_recv()
    sum_b[...] = (acc_b[c].astype(F32) + rx_b0[...].astype(F32)).astype(BF)
    xy_scatter(sum_b, rx_b1, b_s.at[1], b_r.at[1])

    g1[...] = lax.dot_general(s1[0:320, :], d1[...], NT, preferred_element_type=F32)

    def tap_one(b):
        if b > 9:
            return jnp.zeros((16, C1), F32)
        if b == 9:
            return sum(g1[288:304, p * C1 : (p + 1) * C1] for p in range(5))
        return sum(g1[b * 32 + 4 * p : b * 32 + 4 * p + 16, p * C1 : (p + 1) * C1] for p in range(5))

    for g in range(3):
        acc_c[g * 16 : (g + 1) * 16, :] = jnp.concatenate([tap_one(4 * g + i) for i in range(4)], axis=1).astype(BF)
    copy_c0 = pltpu.make_async_remote_copy(
        src_ref=acc_c, dst_ref=rx_c0, send_sem=c_s.at[0], recv_sem=c_r.at[0], device_id=partner, device_id_type=MESH)
    copy_c0.start()
    leaving.append((True, copy_c0.wait_send))
    copy_c0.wait_recv()
    x_c[rank] = (acc_c[...].astype(F32) + rx_c0[...].astype(F32)).astype(BF)
    xy_gather(x_c, c_s.at[1], c_r.at[1])

    @pl.when(owner)
    def _():
        wait_bytes(rx_a1, a_r.at[1])
        z_a[zi] = (sum_a[rank - (rank // 14) * (rank - 13)].astype(F32) + total_of(rx_a1, 15)).astype(BF)
        z_gather(z_a, a_s.at[2], a_r.at[2])

    leaving[-1] = (owner, lambda: wait_bytes(z_a.at[pl.ds(0, 7)], a_s.at[2]))
    wait_bytes(rx_b1, b_r.at[1])
    z_b[zi] = (sum_b[rank].astype(F32) + total_of(rx_b1, 15)).astype(BF)
    z_gather(z_b, b_s.at[2], b_r.at[2])
    half = gath_a.at[c]

    @pl.when(owner)
    def _():
        wait_bytes(z_a.at[pl.ds(0, 7)], a_r.at[2])
        half[rank] = total_of(z_a, 8).astype(BF)
        xy_gather(half, a_s.at[3], a_r.at[3])

    leaving[-1] = (owner, lambda: wait_bytes(gath_a.at[c, pl.ds(0, 15)], a_s.at[3]))
    wait_bytes(x_c.at[pl.ds(0, 15)], c_r.at[1])
    z_c[zi] = total_of(x_c, 16).astype(BF)
    z_gather(z_c, c_s.at[2], c_r.at[2])
    wait_bytes(z_b.at[pl.ds(0, 7)], b_r.at[2])
    half_b = gath_b.at[c]
    half_b[rank] = total_of(z_b, 8).astype(BF)
    xy_gather(half_b, b_s.at[3], b_r.at[3])

    def write(i, src, dst):
        copy = pltpu.make_async_copy(src, dst, outs.at[i])
        copy.start()
        leaving.append((True, copy.wait))

    drain()

    wait_bytes(z_c.at[pl.ds(0, 7)], c_r.at[2])
    fin[...] = total_of(z_c, 8)
    write(0, fin, out_c)

    def to_partner(i, src, dst, send_sem, recv_sem):
        copy = pltpu.make_async_remote_copy(
            src_ref=src, dst_ref=dst, send_sem=send_sem, recv_sem=recv_sem, device_id=partner, device_id_type=MESH)
        copy.start()
        write(i, src, dst)
        leaving.append((True, copy.wait))

    pl.when(owner)(lambda: wait_bytes(half.at[pl.ds(0, 13)], a_r.at[3]))
    pl.when(idle)(lambda: wait_bytes(half.at[pl.ds(0, 14)], a_r.at[3]))
    to_partner(1, half.at[pl.ds(0, 14)], out_a.at[c, pl.ds(0, 14)], a_s.at[4], a_r.at[4])
    wait_bytes(half_b.at[pl.ds(0, 15)], b_r.at[3])
    to_partner(2, half_b, out_b.at[c], b_s.at[4], b_r.at[4])

    drain()


def unpack(in_a, in_b, in_c, o1, ob1, o2, ob2, o3, ob3, gath_a, gath_b, fin, v1, vb1, v2, vb2, v3, vb3, sems, ins):
    pairs = ((in_a.at[0], gath_a.at[0]), (in_a.at[1], gath_a.at[1]), (in_b, gath_b), (in_c, fin))
    loads = [pltpu.make_async_copy(src, dst, ins.at[i]) for i, (src, dst) in enumerate(pairs)]
    for load in loads:
        load.start()
    started = []

    def write(src, dst):
        copy = pltpu.make_async_copy(src, dst, sems.at[len(started)])
        copy.start()
        started.append(copy)

    def rows_b(i):
        return jnp.concatenate([gath_b[0, i].astype(F32), gath_b[1, i].astype(F32)], axis=0)

    for kx in range(3):
        if kx == 0:
            loads[0].wait()
        for t in range(9 * kx, 9 * kx + 9):
            if t == 14:
                loads[1].wait()
            v3[t // 9, (t // 3) % 3, t % 3] = gath_a[t // 14, t % 14].astype(F32)
        write(v3.at[kx], o3.at[kx])
    vb3[...] = gath_a[1, 13].astype(F32)[0:1, :].reshape(C3)
    write(vb3, ob3)
    loads[2].wait()
    for t in range(27):
        i, s = t // 2, (t % 2) * 64
        v2[t // 9, (t // 3) % 3, t % 3] = rows_b(i)[:, s : s + 64]
    write(v2, o2)
    vb2[...] = rows_b(13)[0:1, 64:128].reshape(C2)
    write(vb2, ob2)
    loads[3].wait()
    for b in range(9):
        g, i = b // 4, b % 4
        for kx in range(3):
            v1[kx, b // 3, b % 3] = fin[g * 16 + kx * 4 : g * 16 + kx * 4 + 4, i * 32 : i * 32 + 32]
    write(v1, o1)
    vb1[...] = fin[32:33, 32:64].reshape(C1)
    write(vb1, ob1)
    for copy in started:
        copy.wait()


def local(*args):
    V = pltpu.VMEM
    D = pltpu.SemaphoreType.DMA
    hbm = pl.BlockSpec(memory_space=pltpu.HBM)
    sums = pl.pallas_call(
        body,
        out_shape=(
            jax.ShapeDtypeStruct((2, 16, 64, ZS), BF),
            jax.ShapeDtypeStruct((2, 16, 16, ZS), BF),
            jax.ShapeDtypeStruct((48, ZS), F32),
        ),
        in_specs=[hbm] * 8,
        out_specs=(hbm,) * 3,
        scratch_shapes=[
            V((2, 16, 64, ZS), BF), V((2, 16, 16, ZS), BF), V((48, ZS), F32), D((3,)),
            V((1, C0, 1, YS, ZS), BF), V((3, 3, 3, C0, C1), BF), V((C1,), F32), V((3, 3, 3, C1, C2), BF), V((C2,), F32),
            V((3, 3, 3, C2, C3), BF), V((C3,), F32), D((8,)),
            V((7, C0, YS, ZS), BF), V((1, C3, 1, YS, ZS), BF), V((C3 * YS, ZS), F32), V((256, ZS), F32),
            V((384, ZS), F32), V((160, 384), BF), V((192, 1536), BF), V((C3, 1792), BF), V((192, 1152), BF), V((160, 1792), BF),
            V((ZS, ZS), F32),
            V((384, CELLS), BF), V((1536, CELLS), BF), V((2048, CELLS), BF), V((1152, CELLS), BF), V((1792, CELLS), BF),
            V((160, CELLS), F32), V((192, CELLS), F32), V((C3, CELLS), F32), V((C3, CELLS), BF), V((192, CELLS), BF), V((160, CELLS), BF), V((160, CELLS), F32), V((192, CELLS), F32),
            V((192, CELLS), F32),
            V((896, ZS), BF), V((896, ZS), F32), V((896, ZS), BF), V((14, 64, ZS), BF), V((15, 64, ZS), BF), V((8, 64, ZS), BF),
            V((1472, 192), F32), V((2, 16, 16, ZS), BF), V((16, 16, ZS), BF), V((16, 16, ZS), BF), V((15, 16, ZS), BF), V((8, 16, ZS), BF),
            V((320, 160), F32), V((48, ZS), BF), V((48, ZS), BF), V((16, 48, ZS), BF), V((8, 48, ZS), BF),
            D((7,)), D((7,)), D((5,)), D((5,)), D((5,)), D((5,)), D((3,)), D((3,)), pltpu.SemaphoreType.REGULAR,
        ],
        compiler_params=pltpu.CompilerParams(collective_id=0, has_side_effects=True, vmem_limit_bytes=62 << 20),
        name="backward",
    )(*args)
    shapes = ((3, 3, 3, C0, C1), (C1,), (3, 3, 3, C1, C2), (C2,), (3, 3, 3, C2, C3), (C3,))
    return pl.pallas_call(
        unpack,
        out_shape=tuple(jax.ShapeDtypeStruct(s, F32) for s in shapes),
        in_specs=[hbm] * 3,
        out_specs=(hbm,) * 6,
        scratch_shapes=[V((2, 16, 64, ZS), BF), V((2, 16, 16, ZS), BF), V((48, ZS), F32)]
        + [V(s, F32) for s in shapes]
        + [D((8,)), D((4,))],
        compiler_params=pltpu.CompilerParams(vmem_limit_bytes=62 << 20),
        name="widen",
    )(*sums)


def solution(mesh):
    placed = (
        P("sample", None, "space", None, None),
        P("sample", None, "space", None, None),
        P(), P(), P(), P(), P(), P(),
    )
    return jax.shard_map(local, mesh=mesh, in_specs=placed, out_specs=(P(),) * 6, check_vma=False)
```
